1024 devices in a mesh: gz: 16 (over y, core), blk: 64 (over z, x).
Axes of the slice: x: 4, y: 8, z: 16, core: 2. Of those that a mesh axis runs over, the one named last changes fastest.
Arguments:
- state_old: float32 [16, 64, 4, 5, 4096], P('gz', 'blk'), may hold values from -2 to 8, as said below
- counts_old: int32 [16, 16, 4], replicated, may hold values from 1 to 4, 8 in all within a row
- counts_new: int32 [16, 16, 4], replicated, may hold values from 1 to 4, 8 in all within a row
Outputs:
- state_new: float32 [16, 64, 4, 5, 4096], P('gz', 'blk')
The draws below stay inside these ranges and needn't reach their ends.
Inputs may be any that keep to these rules, and one draw needn't show every extreme that they name: `state_old`: on every cell density and pressure lie in 0.5 to 2 and each velocity component in -1 to 1, in every slot. `counts_old`: in every slab each aligned group of four devices along blk holds exactly 8 meshblocks together, and one device of every group holds 4. `counts_new`: in every slab each aligned group of four devices along blk holds exactly 8 meshblocks together, and one device of every group holds 4.
All inputs are finite; a program needn't handle non-finite values.
Results may differ from the reference program's by a relative error of at most 0.0003.
Values sent between devices are 32-bit elements; how exact they have to be, the bound alone decides.
No kernel may reach another device: no remote copies, remote signals or barrier semaphores. Data moves between devices by JAX's collectives and lax.ppermute only.
A program may use at most 64 MiB of HBM per device.

```python
import math
import jax
import jax.numpy as jnp
import numpy as np
from jax import lax

ROW = 4
BLOCK = 16
SLABS = 16
GROUPS = 16
N_GZ = 16
N_BLK = 64


def draw_state_old(key, part):
    key = jax.random.fold_in(key, 7)
    keys = jax.random.split(key, 4)
    shape = (N_GZ, N_BLK, ROW, BLOCK ** 3)
    lead = (5, N_GZ, N_BLK, ROW, 1)
    cells = jnp.arange(BLOCK ** 3, dtype=jnp.int32)
    x_pos = (cells % BLOCK).astype(jnp.float32)
    y_pos = (cells // BLOCK % BLOCK).astype(jnp.float32)
    z_pos = (cells // (BLOCK * BLOCK)).astype(jnp.float32)
    phase = jax.random.uniform(keys[0], lead, jnp.float32, -3.14159265, 3.14159265)
    sign_y = jnp.where(jax.random.uniform(keys[1], lead, jnp.float32) < 0.5, -1.0, 1.0)
    sign_z = jnp.where(jax.random.uniform(keys[2], lead, jnp.float32) < 0.5, -1.0, 1.0)
    wave = jnp.sin(1.0471976 * (x_pos + sign_y * y_pos + sign_z * z_pos) + phase)
    noise = jnp.clip(0.5 * jax.random.normal(keys[3], (5,) + shape, jnp.float32), -1.0, 1.0)
    mixed = 0.6 * wave + 0.4 * noise
    density = jnp.exp(0.693 * mixed[0])
    velocity = mixed[1:4]
    pressure = jnp.exp(0.693 * mixed[4])
    kinetic = velocity[0] * velocity[0] + velocity[1] * velocity[1] + velocity[2] * velocity[2]
    energy = pressure / 0.4 + 0.5 * density * kinetic
    return jnp.stack([density, density * velocity[0], density * velocity[1], density * velocity[2], energy], axis=3)


def profile(number_of, total, bound, skew):
    weights = [(1 << 20) // math.isqrt(grade ** skew) + 1 for grade in range(2, number_of + 1)]
    rest, given = total - bound - (number_of - 1), [1] * (number_of - 1)
    while rest > 0:
        candidates = [i for i in range(number_of - 1) if given[i] < bound]
        mass, budget = sum([weights[i] for i in candidates]), rest
        for i in candidates:
            addition = min(bound - given[i], max(1, budget * weights[i] // mass), rest)
            given[i] = given[i] + addition
            rest = rest - addition
    return np.array([bound] + given)


def uneven_parts(rng, number_of, total, limit, skew):
    if number_of == 2:
        one = jax.random.randint(rng, (), max(1, total - limit), min(limit, total - 1) + 1)
        return jnp.stack([one, total - one])
    sizes = jnp.asarray(profile(number_of, total, limit, skew), jnp.int32)
    couples = (number_of - 1) // 2
    source_of, sink = sizes[1:1 + 2 * couples:2], sizes[2:2 + 2 * couples:2]
    room = jnp.minimum(source_of - 1, limit - sink)
    passed = jax.random.randint(jax.random.fold_in(rng, 1), (couples,), 0, 1 << 20) % (room + 1)
    sizes = sizes.at[1:1 + 2 * couples:2].set(source_of - passed).at[2:2 + 2 * couples:2].set(sink + passed)
    return sizes[jax.random.permutation(jax.random.fold_in(rng, 2), number_of)]


def setup_inputs(seed: int = 0) -> dict:
    streams_of = jax.random.split(jax.random.key(seed), 4)
    state_old = draw_state_old(jax.random.fold_in(streams_of[3], 71), 0)
    counts_old = jax.vmap(lambda own: uneven_parts(own, 4, 2 * ROW, ROW, 2))(jax.random.split(streams_of[1], SLABS * GROUPS)).reshape((SLABS, GROUPS, 4)).astype(jnp.int32)
    counts_new = jax.vmap(lambda own: uneven_parts(own, 4, 2 * ROW, ROW, 2))(jax.random.split(streams_of[2], SLABS * GROUPS)).reshape((SLABS, GROUPS, 4)).astype(jnp.int32)
    return dict(state_old=state_old, counts_old=counts_old, counts_new=counts_new)


adiabatic_index = 1.4
time_step = 0.08

def limited_slope(left, right):
    return jnp.where(left * right > 0.0, jnp.where(jnp.abs(left) < jnp.abs(right), left, right), 0.0)

def flux_terms(primitive, normal):
    density, velocity_x, velocity_y, velocity_z, pressure = primitive
    speed = (velocity_x, velocity_y, velocity_z)[normal]
    energy = pressure / (adiabatic_index - 1.0) + 0.5 * density * (velocity_x * velocity_x + velocity_y * velocity_y + velocity_z * velocity_z)
    conserved = [density, density * velocity_x, density * velocity_y, density * velocity_z, energy]
    fluxes = [value * speed for value in conserved]
    fluxes[1 + normal] = fluxes[1 + normal] + pressure
    fluxes[4] = fluxes[4] + pressure * speed
    sound = jnp.sqrt(adiabatic_index * pressure / density)
    return (conserved, fluxes, speed, sound)

def wave_flux(left, right, normal):
    left_state, left_flux, left_speed, left_sound = flux_terms(left, normal)
    right_state, right_flux, right_speed, right_sound = flux_terms(right, normal)
    fastest = jnp.maximum(jnp.maximum(left_speed + left_sound, right_speed + right_sound), 0.0)
    slowest = jnp.minimum(jnp.minimum(left_speed - left_sound, right_speed - right_sound), 0.0)
    inverse = 1.0 / (fastest - slowest)
    return [(fastest * left_part - slowest * right_part + fastest * slowest * (right_value - left_value)) * inverse for left_part, right_part, left_value, right_value in zip(left_flux, right_flux, left_state, right_state)]

def rate(conserved, displace):
    density, momentum_x, momentum_y, momentum_z, energy = conserved
    velocity_x = momentum_x / density
    velocity_y = momentum_y / density
    velocity_z = momentum_z / density
    pressure = (adiabatic_index - 1.0) * (energy - 0.5 * (momentum_x * velocity_x + momentum_y * velocity_y + momentum_z * velocity_z))
    primitive = [density, velocity_x, velocity_y, velocity_z, pressure]
    totals = [None] * 5
    for normal in range(3):
        slopes = [limited_slope(value - displace(value, normal, 1), displace(value, normal, -1) - value) for value in primitive]
        left = [value + 0.5 * slope for value, slope in zip(primitive, slopes)]
        right = [displace(value - 0.5 * slope, normal, -1) for value, slope in zip(primitive, slopes)]
        fluxes = wave_flux(left, right, normal)
        for field in range(5):
            change = displace(fluxes[field], normal, 1) - fluxes[field]
            totals[field] = change if normal == 0 else totals[field] + change
    return totals

def starts_of(slab_counts, row_blocks):
    base = jnp.arange(slab_counts.shape[-2], dtype=jnp.int32)[:, None] * (2 * row_blocks)
    return (base + jnp.cumsum(slab_counts, axis=-1) - slab_counts).astype(jnp.int32)

def owner(slab_counts, block_keys, row_blocks):
    group_count = slab_counts.shape[0]
    inclusive = jnp.cumsum(slab_counts, axis=1).astype(jnp.int32)
    exclusive = (inclusive - slab_counts).astype(jnp.int32)
    group = block_keys // (2 * row_blocks)
    local = block_keys - group * (2 * row_blocks)
    pick = (group[..., None] == jnp.arange(group_count, dtype=jnp.int32)).astype(jnp.int32)
    bounds = lax.optimization_barrier(jnp.sum(pick[..., None] * inclusive, axis=-2)).astype(jnp.int32)
    lower = lax.optimization_barrier(jnp.sum(pick[..., None] * exclusive, axis=-2)).astype(jnp.int32)
    position = jnp.minimum(lax.optimization_barrier(jnp.sum((bounds <= local[..., None]).astype(jnp.int32), axis=-1)).astype(jnp.int32), 3)
    first = lax.optimization_barrier(jnp.sum(jnp.where(jnp.arange(4, dtype=jnp.int32) == position[..., None], lower, 0), axis=-1)).astype(jnp.int32)
    return ((group * 4 + position).astype(jnp.int32), (local - first).astype(jnp.int32))

def reference(state_old, counts_old, counts_new):
    plane = ROW * N_BLK // 2
    line_count = N_BLK // 2
    block_keys = jnp.arange(plane, dtype=jnp.int32)
    owner_dev, owner_slot = jax.vmap(lambda slab_counts: owner(slab_counts, block_keys, ROW))(counts_old)
    slab_ids = jnp.arange(N_GZ, dtype=jnp.int32)[:, None]
    blocks = state_old[slab_ids, owner_dev, owner_slot]
    grid = blocks.reshape(N_GZ, line_count, ROW, 5, BLOCK, BLOCK, BLOCK).transpose(3, 0, 4, 1, 5, 2, 6)
    grid = grid.reshape(5, N_GZ * BLOCK, line_count * BLOCK, ROW * BLOCK)
    fields = [grid[field] for field in range(5)]

    def displace(value, normal, amount):
        return jnp.roll(value, amount, axis=2 - normal)
    first = [value + time_step * change for value, change in zip(fields, rate(fields, displace))]
    second = [0.5 * value + 0.5 * (middle + time_step * change) for value, middle, change in zip(fields, first, rate(first, displace))]
    final = jnp.stack(second).reshape(5, N_GZ, BLOCK, line_count, BLOCK, ROW, BLOCK)
    final = final.transpose(1, 3, 5, 0, 2, 4, 6).reshape(N_GZ, plane, 5, BLOCK ** 3)
    starts = starts_of(counts_new, ROW).reshape(N_GZ, N_BLK)
    slot_ids = jnp.arange(ROW, dtype=jnp.int32)
    new_keys = ((starts[:, :, None] + slot_ids) % plane).astype(jnp.int32)
    valid = slot_ids < counts_new.reshape(N_GZ, N_BLK)[:, :, None]
    placed = final[jnp.arange(N_GZ, dtype=jnp.int32)[:, None, None], new_keys]
    return jnp.where(valid[..., None, None], placed, 0.0)
```

```python
import jax
import jax.numpy as jnp
from jax import lax
from jax.experimental import pallas as pl
from jax.experimental.pallas import tpu as pltpu
from jax.sharding import PartitionSpec as P


FIELDS = 5
GROUP = 4
SLOTS = 4
KEYS = 8
ROWS = 8
LANES = 128
QUARTER = 4
HALO = 4

TIME_STEP = 0.08
GAMMA = 1.4

VMEM = pl.BlockSpec(memory_space=pltpu.VMEM)
SMEM = pl.BlockSpec(memory_space=pltpu.SMEM)


def call(kernel, out_shapes, in_specs, scratch=(), flops=0, data=1 << 20):
    return pl.pallas_call(
        kernel,
        out_shape=out_shapes,
        in_specs=in_specs,
        out_specs=jax.tree.map(lambda _: VMEM, out_shapes),
        scratch_shapes=list(scratch),
        compiler_params=pltpu.CompilerParams(vmem_limit_bytes=24 << 20),
        cost_estimate=pl.CostEstimate(flops=flops, bytes_accessed=data, transcendentals=0),
    )


def f32(*shape):
    return jax.ShapeDtypeStruct(shape, jnp.float32)


def split_kernel(state, message):
    for slot in range(SLOTS):
        for part in range(GROUP):
            for row in range(ROWS):
                chunk = (part * ROWS + row) * LANES
                message[part, slot, :, row, :] = state[slot, :, chunk : chunk + LANES]


def place_of(counts, key):
    position = jnp.int32(0)
    first = jnp.int32(0)
    upto = jnp.int32(0)
    for device in range(GROUP - 1):
        upto = upto + counts[device]
        beyond = upto <= key
        position = position + beyond.astype(jnp.int32)
        first = jnp.where(beyond, upto, first)
    return position, jnp.clip(key - first, 0, SLOTS - 1)


def edge_kernel(counts, received, lower, upper):
    for out, block_y, half in ((lower, 0, 0), (upper, 1, 1)):
        for xb in range(4):
            device, slot = place_of(counts, block_y * 4 + xb)
            to = (xb % 2) * 4
            for field in range(FIELDS):
                out[field, xb // 2, to : to + 4, :] = received[
                    device, slot, field, pl.ds(half, 4, stride=2), :
                ]


def gather_kernel(counts, received, from_above, from_below, piece):
    for block_y in range(2):
        for xb in range(4):
            device, slot = place_of(counts, block_y * 4 + xb)
            for field in range(FIELDS):
                for z in range(QUARTER):
                    piece[field, z * 2 + block_y, 2 * xb : 2 * xb + 2, :] = received[
                        device, slot, field, 2 * z : 2 * z + 2, :
                    ]
    lane = lax.broadcasted_iota(jnp.int32, (FIELDS, 2, ROWS, LANES), 3)
    piece[:, 8:10] = jnp.where(lane < 64, from_above[...], from_below[...])


def minmod(left, right):
    return jnp.maximum(jnp.minimum(left, right), 0.0) + jnp.minimum(jnp.maximum(left, right), 0.0)


def primitives(conserved):
    density, mx, my, mz, energy = conserved
    inverse = 1.0 / density
    vx, vy, vz = mx * inverse, my * inverse, mz * inverse
    pressure = (GAMMA - 1.0) * (energy - 0.5 * (mx * vx + my * vy + mz * vz))
    return [density, vx, vy, vz, pressure]


def face_terms(primitive, normal):
    density, vx, vy, vz, pressure = primitive
    energy = pressure * (1.0 / (GAMMA - 1.0)) + (0.5 * density) * (vx * vx + vy * vy + vz * vz)
    conserved = [density, density * vx, density * vy, density * vz, energy]
    stiff = GAMMA * pressure
    sound = stiff * lax.rsqrt(stiff * density)
    return conserved, primitive[1 + normal], pressure, sound


def face_flux(left, right, normal):
    left_u, left_v, left_p, left_c = face_terms(left, normal)
    right_u, right_v, right_p, right_c = face_terms(right, normal)
    fastest = jnp.maximum(jnp.maximum(left_v + left_c, right_v + right_c), 0.0)
    slowest = jnp.minimum(jnp.minimum(left_v - left_c, right_v - right_c), 0.0)
    inverse = 1.0 / (fastest - slowest)
    plus = fastest * inverse
    minus = slowest * inverse
    left_weight = plus * (left_v - slowest)
    right_weight = minus * (right_v - fastest)
    left_push = plus * left_p
    right_push = minus * right_p
    fluxes = [left_weight * a - right_weight * b for a, b in zip(left_u, right_u)]
    fluxes[1 + normal] = fluxes[1 + normal] + (left_push - right_push)
    fluxes[4] = fluxes[4] + (left_push * left_v - right_push * right_v)
    return fluxes


def shift_x(value, amount):
    axis = value.ndim - 1
    x = lax.broadcasted_iota(jnp.int32, value.shape, axis) % 16
    if amount > 0:
        inner = pltpu.roll(value, 1, axis)
        outer = pltpu.roll(pltpu.roll(value, 2, axis - 1), LANES - 15, axis)
        return jnp.where(x == 0, outer, inner)
    inner = pltpu.roll(value, LANES - 1, axis)
    outer = pltpu.roll(pltpu.roll(value, ROWS - 2, axis - 1), 15, axis)
    return jnp.where(x == 15, outer, inner)


def shift_y(value, amount):
    lane = lax.broadcasted_iota(jnp.int32, (ROWS, LANES), 1)
    odd = lax.broadcasted_iota(jnp.int32, (ROWS, LANES), 0) % 2 == 1
    if amount > 0:
        moved = [pltpu.roll(v, 16, 1) for v in value]
        edge = [
            jnp.where(odd, pltpu.roll(moved[i], 1, 0), pltpu.roll(moved[i - 1], ROWS - 1, 0))
            for i in range(3)
        ]
        return [jnp.where(lane < 16, e, m) for e, m in zip(edge, moved)]
    moved = [pltpu.roll(v, LANES - 16, 1) for v in value]
    edge = [
        jnp.where(odd, pltpu.roll(moved[(i + 1) % 3], 1, 0), pltpu.roll(moved[i], ROWS - 1, 0))
        for i in range(3)
    ]
    return [jnp.where(lane >= LANES - 16, e, m) for e, m in zip(edge, moved)]


def sweep_x(primitive):
    ahead = [shift_x(q, -1) for q in primitive]
    steps = [b - q for q, b in zip(primitive, ahead)]
    half = [0.5 * minmod(shift_x(d, 1), d) for d in steps]
    left = [q + h for q, h in zip(primitive, half)]
    right = [shift_x(q - h, -1) for q, h in zip(primitive, half)]
    return [shift_x(f, 1) - f for f in face_flux(left, right, 0)]


def sweep_y(primitive):
    left, right = [], []
    for q in primitive:
        ahead = shift_y(q, -1)
        steps = [b - a for a, b in zip(q, ahead)]
        behind = shift_y(steps, 1)
        half = [0.5 * minmod(b, d) for b, d in zip(behind, steps)]
        left.append([a + h for a, h in zip(q, half)])
        right.append(shift_y([a - h for a, h in zip(q, half)], -1))
    fluxes = [face_flux([l[i] for l in left], [r[i] for r in right], 1) for i in range(3)]
    out = []
    for field in range(FIELDS):
        flux = [fluxes[i][field] for i in range(3)]
        out.append([b - f for b, f in zip(shift_y(flux, 1), flux)])
    return out


def rate_into(total, prim, count, width):
    def plane(z, carry):
        for i in range(width):
            values = [prim[f, z + 2, i] for f in range(FIELDS)]
            for f, change in enumerate(sweep_x(values)):
                total[f, z, i] = change
        changes = sweep_y([[prim[f, z + 2, i] for i in range(3)] for f in range(FIELDS)])
        for f in range(FIELDS):
            for i in range(width):
                total[f, z, i] = total[f, z, i] + changes[f][i]
        return carry

    lax.fori_loop(0, count, plane, 0)

    for i in range(width):
        here = [prim[f, 1, i] for f in range(FIELDS)]
        step = [h - prim[f, 0, i] for f, h in enumerate(here)]
        ahead = [prim[f, 2, i] for f in range(FIELDS)]
        ahead_step = [a - h for a, h in zip(ahead, here)]
        half = [0.5 * minmod(a, b) for a, b in zip(step, ahead_step)]

        def face(z, state):
            here, half, ahead, ahead_step, below = state
            beyond = [prim[f, z + 3, i] for f in range(FIELDS)]
            beyond_step = [b - a for a, b in zip(ahead, beyond)]
            ahead_half = [0.5 * minmod(a, b) for a, b in zip(ahead_step, beyond_step)]
            left = [q + h for q, h in zip(here, half)]
            right = [q - h for q, h in zip(ahead, ahead_half)]
            fluxes = face_flux(left, right, 2)
            return (ahead, ahead_half, beyond, beyond_step, fluxes)

        state = face(0, (here, half, ahead, ahead_step, None))

        def layer(z, state):
            below = state[4]
            state = face(z + 1, state)
            for f in range(FIELDS):
                total[f, z, i] = total[f, z, i] + (below[f] - state[4][f])
            return state

        lax.fori_loop(0, count, layer, state)


def advance_kernel(counts, low, own, high, message, u0, w0, u1, w1, change, done):
    for base, piece in ((0, low), (QUARTER, own), (2 * QUARTER, high)):
        for field in range(FIELDS):
            for z in range(QUARTER):
                for block_y in range(2):
                    u0[field, base + z, block_y] = piece[field, z * 2 + block_y]
                for xb in range(4):
                    row = (xb % 2) * 4 + z
                    halo = piece[field, 8 + xb // 2, row : row + 1, :]
                    u0[field, base + z, 2, 2 * xb : 2 * xb + 2, :] = jnp.broadcast_to(
                        halo, (2, LANES)
                    )

    def to_primitive(z, carry):
        for f, value in enumerate(primitives([u0[f, z] for f in range(FIELDS)])):
            w0[f, z] = value
        return carry

    lax.fori_loop(0, QUARTER + 2 * HALO, to_primitive, 0)
    rate_into(change, w0, QUARTER + HALO, 3)

    def first_step(z, carry):
        values = [u0[f, z + 2] + TIME_STEP * change[f, z] for f in range(FIELDS)]
        for f, value in enumerate(values):
            u1[f, z] = value
        for f, value in enumerate(primitives(values)):
            w1[f, z] = value
        return carry

    lax.fori_loop(0, QUARTER + HALO, first_step, 0)
    rate_into(change, w1, QUARTER, 2)

    for z in range(QUARTER):
        for field in range(FIELDS):
            for block_y in range(2):
                value = 0.5 * u0[field, z + HALO, block_y] + 0.5 * (
                    u1[field, z + 2, block_y] + TIME_STEP * change[field, z, block_y]
                )
                for xb in range(4):
                    done[block_y * 4 + xb, field, 2 * z : 2 * z + 2, :] = value[
                        2 * xb : 2 * xb + 2, :
                    ]

    start = jnp.int32(0)
    for device in range(GROUP):
        for slot in range(SLOTS):
            message[device, slot] = done[jnp.minimum(start + slot, KEYS - 1)]
        start = start + counts[device]


def join_kernel(count, received, state):
    for slot in range(SLOTS):
        valid = slot < count[0]
        for part in range(GROUP):
            for row in range(ROWS):
                chunk = (part * ROWS + row) * LANES
                value = received[part, slot, :, row, :]
                state[slot, :, chunk : chunk + LANES] = jnp.where(valid, value, 0.0)


def body(state_old, counts_old, counts_new):
    slabs = lax.axis_size("gz")
    places = lax.axis_size("blk")
    groups = places // GROUP
    slab = lax.axis_index("gz")
    place = lax.axis_index("blk")
    group = place // GROUP

    def row_of(counts):
        return lax.dynamic_slice(counts, (slab, group, 0), (1, 1, GROUP)).reshape(GROUP)

    old_here = row_of(counts_old)
    new_here = row_of(counts_new)
    count_here = lax.dynamic_slice(new_here, (place % GROUP,), (1,))
    members = [[g * GROUP + k for k in range(GROUP)] for g in range(groups)]

    def exchange(message):
        return lax.all_to_all(message, "blk", 0, 0, axis_index_groups=members)

    def along_y(value, by):
        route = [(i, (i + by * GROUP) % places) for i in range(places)]
        return lax.ppermute(value, "blk", route)

    def along_z(value, by):
        route = []
        for g in range(slabs):
            for i in range(places):
                layer = (g * GROUP + i % GROUP + by) % (slabs * GROUP)
                target = layer // GROUP * places + i // GROUP * GROUP + layer % GROUP
                route.append((g * places + i, target))
        return lax.ppermute(value, ("gz", "blk"), route)

    parts = f32(GROUP, SLOTS, FIELDS, ROWS, LANES)
    held = state_old.reshape(SLOTS, FIELDS, GROUP * ROWS * LANES)
    sent = call(split_kernel, parts, [VMEM])(held)
    received = exchange(sent)

    edge = f32(FIELDS, 2, ROWS, LANES)
    lower, upper = call(edge_kernel, [edge, edge], [SMEM, VMEM])(old_here, received)
    from_above = along_y(lower, -1)
    from_below = along_y(upper, 1)
    own = call(gather_kernel, f32(FIELDS, 10, ROWS, LANES), [SMEM, VMEM, VMEM, VMEM])(
        old_here, received, from_above, from_below
    )
    low = along_z(own, 1)
    high = along_z(own, -1)

    def work(layers):
        return pltpu.VMEM((FIELDS, layers, 3, ROWS, LANES), jnp.float32)

    deep, wide = QUARTER + 2 * HALO, QUARTER + HALO
    finished = call(
        advance_kernel,
        parts,
        [SMEM, VMEM, VMEM, VMEM],
        [work(deep), work(deep), work(wide), work(wide), work(wide)]
        + [pltpu.VMEM((KEYS, FIELDS, ROWS, LANES), jnp.float32)],
        flops=1 << 24,
    )(new_here, low, own, high)
    returned = exchange(finished)
    state = call(join_kernel, f32(SLOTS, FIELDS, GROUP * ROWS * LANES), [SMEM, VMEM])(
        count_here, returned
    )
    return state[None, None]


def solution(mesh):
    in_specs = (P("gz", "blk", None, None, None), P(), P())
    out_specs = P("gz", "blk", None, None, None)
    return jax.shard_map(body, mesh=mesh, in_specs=in_specs, out_specs=out_specs, check_vma=False)
```

```python
import jax
import jax.numpy as jnp
from jax import lax
from jax.experimental import pallas as pl
from jax.experimental.pallas import tpu as pltpu
from jax.sharding import PartitionSpec as P


FIELDS = 5
GROUP = 4
SLOTS = 4
KEYS = 8
ROWS = 8
LANES = 128
QUARTER = 4
HALO = 4

TIME_STEP = 0.08
GAMMA = 1.4

VMEM = pl.BlockSpec(memory_space=pltpu.VMEM)
SMEM = pl.BlockSpec(memory_space=pltpu.SMEM)


def call(kernel, out_shapes, in_specs, scratch=(), flops=0, data=1 << 20):
    return pl.pallas_call(
        kernel,
        out_shape=out_shapes,
        in_specs=in_specs,
        out_specs=jax.tree.map(lambda _: VMEM, out_shapes),
        scratch_shapes=list(scratch),
        compiler_params=pltpu.CompilerParams(vmem_limit_bytes=24 << 20),
        cost_estimate=pl.CostEstimate(flops=flops, bytes_accessed=data, transcendentals=0),
    )


def f32(*shape):
    return jax.ShapeDtypeStruct(shape, jnp.float32)


def split_kernel(state, message):
    for field in range(FIELDS):
        for part in range(GROUP):
            for row in range(ROWS):
                chunk = (part * ROWS + row) * LANES
                message[part, field, 4 * row : 4 * row + 4, :] = state[
                    field, :, chunk : chunk + LANES
                ]


def place_of(counts, key):
    position = jnp.int32(0)
    first = jnp.int32(0)
    upto = jnp.int32(0)
    for device in range(GROUP - 1):
        upto = upto + counts[device]
        beyond = upto <= key
        position = position + beyond.astype(jnp.int32)
        first = jnp.where(beyond, upto, first)
    return position, jnp.clip(key - first, 0, SLOTS - 1)


def gather_kernel(counts, received, piece):
    for block_y in range(2):
        for xb in range(4):
            device, slot = place_of(counts, block_y * 4 + xb)
            for field in range(FIELDS):
                block = received[device, field, pl.ds(slot, ROWS, stride=SLOTS), :]
                for z in range(QUARTER):
                    piece[field, z * 2 + block_y, 2 * xb : 2 * xb + 2, :] = block[
                        2 * z : 2 * z + 2
                    ]


def layers_of(low, own, high):
    return [(low, 2), (low, 3)] + [(own, z) for z in range(QUARTER)] + [(high, 0), (high, 1)]


def edge_kernel(low, own, high, lower, upper):
    layers = layers_of(low, own, high)
    first_half = lax.broadcasted_iota(jnp.int32, (4, LANES), 1) < 64
    for field in range(FIELDS):
        for pair in range(4):
            to = (pair % 2) * 4

            def rows(index, block_y):
                piece, z = layers[index]
                return piece[field, z * 2 + block_y, pl.ds(block_y, 4, stride=2), :]

            lower[field, pair // 2, to : to + 4, :] = jnp.where(
                first_half, rows(pair, 0), pltpu.roll(rows(pair + 4, 0), 64, 1)
            )
            upper[field, pair // 2, to : to + 4, :] = jnp.where(
                first_half, pltpu.roll(rows(pair, 1), 64, 1), rows(pair + 4, 1)
            )


def minmod(left, right):
    return jnp.maximum(jnp.minimum(left, right), 0.0) + jnp.minimum(jnp.maximum(left, right), 0.0)


def primitives(conserved):
    density, mx, my, mz, energy = conserved
    inverse = 1.0 / density
    vx, vy, vz = mx * inverse, my * inverse, mz * inverse
    pressure = (GAMMA - 1.0) * (energy - 0.5 * (mx * vx + my * vy + mz * vz))
    return [density, vx, vy, vz, pressure]


def face_terms(primitive, normal):
    density, vx, vy, vz, pressure = primitive
    energy = pressure * (1.0 / (GAMMA - 1.0)) + (0.5 * density) * (vx * vx + vy * vy + vz * vz)
    conserved = [density, density * vx, density * vy, density * vz, energy]
    stiff = GAMMA * pressure
    sound = stiff * lax.rsqrt(stiff * density)
    return conserved, primitive[1 + normal], pressure, sound


def face_flux(left, right, normal):
    left_u, left_v, left_p, left_c = face_terms(left, normal)
    right_u, right_v, right_p, right_c = face_terms(right, normal)
    fastest = jnp.maximum(jnp.maximum(left_v + left_c, right_v + right_c), 0.0)
    slowest = jnp.minimum(jnp.minimum(left_v - left_c, right_v - right_c), 0.0)
    inverse = 1.0 / (fastest - slowest)
    plus = fastest * inverse
    minus = slowest * inverse
    left_weight = plus * (left_v - slowest)
    right_weight = minus * (right_v - fastest)
    left_push = plus * left_p
    right_push = minus * right_p
    fluxes = [left_weight * a - right_weight * b for a, b in zip(left_u, right_u)]
    fluxes[1 + normal] = fluxes[1 + normal] + (left_push - right_push)
    fluxes[4] = fluxes[4] + (left_push * left_v - right_push * right_v)
    return fluxes


def shift_x(value, amount):
    axis = value.ndim - 1
    x = lax.broadcasted_iota(jnp.int32, value.shape, axis) % 16
    if amount > 0:
        inner = pltpu.roll(value, 1, axis)
        outer = pltpu.roll(pltpu.roll(value, 2, axis - 1), LANES - 15, axis)
        return jnp.where(x == 0, outer, inner)
    inner = pltpu.roll(value, LANES - 1, axis)
    outer = pltpu.roll(pltpu.roll(value, ROWS - 2, axis - 1), 15, axis)
    return jnp.where(x == 15, outer, inner)


def shift_y(value, amount):
    shape = value[0].shape
    across, down = len(shape) - 1, len(shape) - 2
    lane = lax.broadcasted_iota(jnp.int32, shape, across)
    odd = lax.broadcasted_iota(jnp.int32, shape, down) % 2 == 1
    if amount > 0:
        moved = [pltpu.roll(v, 16, across) for v in value]
        upper = moved
        lower = [moved[i - 1] for i in range(3)]
        outer = lane < 16
    else:
        moved = [pltpu.roll(v, LANES - 16, across) for v in value]
        upper = [moved[(i + 1) % 3] for i in range(3)]
        lower = moved
        outer = lane >= LANES - 16
    edge = [
        jnp.where(odd, pltpu.roll(u, 1, down), pltpu.roll(l, ROWS - 1, down))
        for u, l in zip(upper, lower)
    ]
    return [jnp.where(outer, e, m) for e, m in zip(edge, moved)]


def sweep_x(primitive):
    ahead = [shift_x(q, -1) for q in primitive]
    steps = [b - q for q, b in zip(primitive, ahead)]
    half = [0.5 * minmod(shift_x(d, 1), d) for d in steps]
    left = [q + h for q, h in zip(primitive, half)]
    right = [shift_x(q - h, -1) for q, h in zip(primitive, half)]
    return [shift_x(f, 1) - f for f in face_flux(left, right, 0)]


def sweep_y(primitive):
    left, right = [], []
    for q in primitive:
        ahead = shift_y(q, -1)
        steps = [b - a for a, b in zip(q, ahead)]
        behind = shift_y(steps, 1)
        half = [0.5 * minmod(b, d) for b, d in zip(behind, steps)]
        left.append([a + h for a, h in zip(q, half)])
        right.append(shift_y([a - h for a, h in zip(q, half)], -1))
    fluxes = [face_flux([l[i] for l in left], [r[i] for r in right], 1) for i in range(3)]
    out = []
    for field in range(FIELDS):
        flux = [fluxes[i][field] for i in range(3)]
        out.append([b - f for b, f in zip(shift_y(flux, 1), flux)])
    return out


X_LAYERS = 4
Y_LAYERS = 4


def rate_x(total, prim, count, blocks):
    def planes(step, carry):
        z = step * X_LAYERS
        values = [prim[f, pl.ds(z + 2, X_LAYERS), blocks] for f in range(FIELDS)]
        for f, change in enumerate(sweep_x(values)):
            total[f, pl.ds(z, X_LAYERS), blocks] = change
        return carry

    lax.fori_loop(0, count // X_LAYERS, planes, 0)


def rate_z(total, prim, count, blocks):
    def load(z):
        return [prim[f, z, blocks] for f in range(FIELDS)]

    here, ahead = load(1), load(2)
    step = [h - b for h, b in zip(here, load(0))]
    ahead_step = [a - h for a, h in zip(ahead, here)]
    half = [0.5 * minmod(a, b) for a, b in zip(step, ahead_step)]

    def face(z, here, half, ahead, ahead_step):
        beyond = load(z + 3)
        beyond_step = [b - a for a, b in zip(ahead, beyond)]
        ahead_half = [0.5 * minmod(a, b) for a, b in zip(ahead_step, beyond_step)]
        left = [q + h for q, h in zip(here, half)]
        right = [q - h for q, h in zip(ahead, ahead_half)]
        return ahead, ahead_half, beyond, beyond_step, face_flux(left, right, 2)

    def layer(z, state):
        after = face(z + 1, *state[:4])
        for f in range(FIELDS):
            total[f, z, blocks] = total[f, z, blocks] + (state[4][f] - after[4][f])
        return after

    lax.fori_loop(0, count, layer, face(0, here, half, ahead, ahead_step))


INNER = slice(0, 2)
EDGE = slice(2, 3)


def inner_kernel(low, own, high, w0, change):
    for base, piece in ((0, low), (QUARTER, own), (2 * QUARTER, high)):

        def to_primitive(z, carry):
            values = [piece[f, pl.ds(2 * z, 2)] for f in range(FIELDS)]
            for f, value in enumerate(primitives(values)):
                w0[f, base + z] = value
            return carry

        lax.fori_loop(0, QUARTER, to_primitive, 0)
    rate_x(change, w0, QUARTER + HALO, INNER)
    rate_z(change, w0, QUARTER + HALO, INNER)


def advance_kernel(
    counts, low, own, high, w0, inner, from_above, from_below, message,
    uh, wh, changeh, total, u1, w1, change, done,
):
    wide = QUARTER + HALO
    first_half = lax.broadcasted_iota(jnp.int32, (4, LANES), 1) < 64
    for field in range(FIELDS):
        for pair in range(4):
            rows = slice((pair % 2) * 4, (pair % 2) * 4 + 4)
            above = from_above[field, pair // 2, rows, :]
            below = from_below[field, pair // 2, rows, :]
            for z, halo in (
                (pair, jnp.where(first_half, above, pltpu.roll(below, 64, 1))),
                (pair + 4, jnp.where(first_half, pltpu.roll(above, 64, 1), below)),
            ):
                uh[field, z, 0, pl.ds(0, 4, stride=2), :] = halo
                uh[field, z, 0, pl.ds(1, 4, stride=2), :] = halo
    for f, value in enumerate(primitives([uh[f] for f in range(FIELDS)])):
        wh[f] = value

    rate_x(changeh, wh, QUARTER, slice(0, 1))
    rate_z(changeh, wh, QUARTER, slice(0, 1))

    def planes(step, carry):
        z = step * Y_LAYERS
        here, shifted = pl.ds(z, Y_LAYERS), pl.ds(z + 2, Y_LAYERS)
        prims = [[w0[f, shifted, 0], w0[f, shifted, 1], wh[f, here, 0]] for f in range(FIELDS)]
        changes = sweep_y(prims)
        for f in range(FIELDS):
            for i in range(2):
                total[f, here, i] = inner[f, here, i] + changes[f][i]
            total[f, here, 2] = changes[f][2]
        return carry

    lax.fori_loop(0, wide // Y_LAYERS, planes, 0)

    for index, (piece, z) in enumerate(layers_of(low, own, high)):
        values = [
            piece[f, 2 * z : 2 * z + 2] + TIME_STEP * total[f, index, INNER]
            for f in range(FIELDS)
        ]
        for f, value in enumerate(values):
            u1[f, index] = value
        for f, value in enumerate(primitives(values)):
            w1[f, index, INNER] = value
    for z in range(QUARTER):
        values = [
            uh[f, z + 2] + TIME_STEP * (total[f, z + 2, EDGE] + changeh[f, z])
            for f in range(FIELDS)
        ]
        for f, value in enumerate(primitives(values)):
            w1[f, z + 2, EDGE] = value

    rate_x(change, w1, QUARTER, INNER)
    rate_z(change, w1, QUARTER, INNER)

    def last_planes(step, carry):
        z = step * Y_LAYERS
        here, shifted = pl.ds(z, Y_LAYERS), pl.ds(z + 2, Y_LAYERS)
        changes = sweep_y([[w1[f, shifted, i] for i in range(3)] for f in range(FIELDS)])
        for f in range(FIELDS):
            for i in range(2):
                change[f, here, i] = change[f, here, i] + changes[f][i]
        return carry

    lax.fori_loop(0, QUARTER // Y_LAYERS, last_planes, 0)

    for z in range(QUARTER):
        for field in range(FIELDS):
            for block_y in range(2):
                value = 0.5 * own[field, 2 * z + block_y] + 0.5 * (
                    u1[field, z + 2, block_y] + TIME_STEP * change[field, z, block_y]
                )
                for xb in range(4):
                    done[block_y * 4 + xb, field, 2 * z : 2 * z + 2, :] = value[
                        2 * xb : 2 * xb + 2, :
                    ]

    start = jnp.int32(0)
    for device in range(GROUP):
        for slot in range(SLOTS):
            key = jnp.minimum(start + slot, KEYS - 1)
            for field in range(FIELDS):
                message[device, field, pl.ds(slot, ROWS, stride=SLOTS), :] = done[key, field]
        start = start + counts[device]


def join_kernel(count, received, state):
    valid = lax.broadcasted_iota(jnp.int32, (SLOTS, LANES), 0) < count[0]
    for field in range(FIELDS):
        for part in range(GROUP):
            for row in range(ROWS):
                chunk = (part * ROWS + row) * LANES
                state[field, :, chunk : chunk + LANES] = jnp.where(
                    valid, received[part, field, 4 * row : 4 * row + 4, :], 0.0
                )


def body(state_old, counts_old, counts_new):
    slabs = lax.axis_size("gz")
    places = lax.axis_size("blk")
    groups = places // GROUP
    slab = lax.axis_index("gz")
    place = lax.axis_index("blk")
    group = place // GROUP

    def row_of(counts):
        return lax.dynamic_slice(counts, (slab, group, 0), (1, 1, GROUP)).reshape(GROUP)

    old_here = row_of(counts_old)
    new_here = row_of(counts_new)
    count_here = lax.dynamic_slice(new_here, (place % GROUP,), (1,))
    members = [[g * GROUP + k for k in range(GROUP)] for g in range(groups)]

    def exchange(message):
        return lax.all_to_all(message, "blk", 0, 0, axis_index_groups=members)

    def along_y(value, by):
        route = [(i, (i + by * GROUP) % places) for i in range(places)]
        return lax.ppermute(value, "blk", route)

    def along_z(value, by):
        route = []
        for g in range(slabs):
            for i in range(places):
                layer = (g * GROUP + i % GROUP + by) % (slabs * GROUP)
                target = layer // GROUP * places + i // GROUP * GROUP + layer % GROUP
                route.append((g * places + i, target))
        return lax.ppermute(value, ("gz", "blk"), route)

    parts = f32(GROUP, FIELDS, ROWS * SLOTS, LANES)
    cells = GROUP * ROWS * LANES
    wide = QUARTER + HALO
    held = state_old.reshape(SLOTS, FIELDS, cells).transpose(1, 0, 2)
    received = exchange(call(split_kernel, parts, [VMEM])(held))

    own = call(gather_kernel, f32(FIELDS, 2 * QUARTER, ROWS, LANES), [SMEM, VMEM])(
        old_here, received
    )
    low = along_z(own, 1)
    high = along_z(own, -1)

    edge = f32(FIELDS, 2, ROWS, LANES)
    lower, upper = call(edge_kernel, [edge, edge], [VMEM] * 3)(low, own, high)
    from_above = along_y(lower, -1)
    from_below = along_y(upper, 1)
    w0, inner = call(
        inner_kernel,
        [f32(FIELDS, wide + HALO, 2, ROWS, LANES), f32(FIELDS, wide, 2, ROWS, LANES)],
        [VMEM] * 3,
        flops=1 << 24,
    )(low, own, high)

    def work(*shape):
        return pltpu.VMEM((FIELDS,) + shape + (ROWS, LANES), jnp.float32)

    finished = call(
        advance_kernel,
        parts,
        [SMEM] + [VMEM] * 7,
        [work(wide, 1), work(wide, 1), work(QUARTER, 1), work(wide, 3)]
        + [work(wide, 2), work(wide, 3), work(QUARTER, 2)]
        + [pltpu.VMEM((KEYS, FIELDS, ROWS, LANES), jnp.float32)],
        flops=1 << 24,
    )(new_here, low, own, high, w0, inner, from_above, from_below)
    returned = exchange(finished)
    state = call(join_kernel, f32(FIELDS, SLOTS, cells), [SMEM, VMEM])(count_here, returned)
    return state.transpose(1, 0, 2)[None, None]


def solution(mesh):
    in_specs = (P("gz", "blk", None, None, None), P(), P())
    out_specs = P("gz", "blk", None, None, None)
    return jax.shard_map(body, mesh=mesh, in_specs=in_specs, out_specs=out_specs, check_vma=False)
```

```python
import jax
import jax.numpy as jnp
from jax import lax
from jax.experimental import pallas as pl
from jax.experimental.pallas import tpu as pltpu
from jax.sharding import PartitionSpec as P


FIELDS = 5
GROUP = 4
SLOTS = 4
KEYS = 8
ROWS = 8
LANES = 128
HALO = 4
DEPTH = 16
WIDE = DEPTH + HALO
DEEP = DEPTH + 2 * HALO

TIME_STEP = 0.08
GAMMA = 1.4

VMEM = pl.BlockSpec(memory_space=pltpu.VMEM)
SMEM = pl.BlockSpec(memory_space=pltpu.SMEM)


def call(kernel, out_shapes, in_specs, scratch=(), flops=0, data=1 << 20):
    return pl.pallas_call(
        kernel,
        out_shape=out_shapes,
        in_specs=in_specs,
        out_specs=jax.tree.map(lambda _: VMEM, out_shapes),
        scratch_shapes=list(scratch),
        compiler_params=pltpu.CompilerParams(vmem_limit_bytes=24 << 20),
        cost_estimate=pl.CostEstimate(flops=flops, bytes_accessed=data, transcendentals=0),
    )


def f32(*shape):
    return jax.ShapeDtypeStruct(shape, jnp.float32)


def place_of(counts, key):
    position = jnp.int32(0)
    first = jnp.int32(0)
    upto = jnp.int32(0)
    for device in range(GROUP - 1):
        upto = upto + counts[device]
        beyond = upto <= key
        position = position + beyond.astype(jnp.int32)
        first = jnp.where(beyond, upto, first)
    return position, jnp.clip(key - first, 0, SLOTS - 1)


def arrange(counts, received, part, piece, base):
    for block_y in range(2):
        for xb in range(4):
            device, slot = place_of(counts, block_y * 4 + xb)
            start = part * (SLOTS * ROWS) + slot
            for field in range(FIELDS):
                block = received[device, field, pl.ds(start, ROWS, stride=SLOTS), :]
                for z in range(HALO):
                    piece[field, base + z * 2 + block_y, 2 * xb : 2 * xb + 2, :] = block[
                        2 * z : 2 * z + 2
                    ]


def even_slab():
    return lax.axis_index("gz") % 2 == 0


def outer_kernel(counts, received, near, far):
    even = even_slab()
    top, bottom = DEPTH // HALO - 1, 0
    arrange(counts, received, jnp.where(even, top, bottom), near, 0)
    arrange(counts, received, jnp.where(even, bottom, top), far, 0)


def own_kernel(counts, received, own, prim, change):
    for part in range(DEPTH // HALO):
        arrange(counts, received, part, own, part * 2 * HALO)

    def to_primitive(z, carry):
        values = [own[f, pl.ds(4 * z, 4)] for f in range(FIELDS)]
        for f, value in enumerate(primitives(values)):
            prim[f, pl.ds(2 * z, 2), 0] = jnp.stack([value[0], value[2]])
            prim[f, pl.ds(2 * z, 2), 1] = jnp.stack([value[1], value[3]])
        return carry

    lax.fori_loop(0, DEPTH // 2, to_primitive, 0)
    rate_x(change, prim, 0, 0, DEPTH, INNER)


def below_above(near, far, index):
    even = even_slab()
    return jnp.where(even, far[index], near[index]), jnp.where(even, near[index], far[index])


def edge_kernel(near, far, own, lower, upper):
    first_half = lax.broadcasted_iota(jnp.int32, (4, LANES), 1) < 64
    even = even_slab()
    pairs = WIDE // 2

    def rows(field, layer, block_y):
        rest = pl.ds(block_y, 4, stride=2)
        if layer < 0:
            at = (field, 2 * (layer + HALO) + block_y, rest)
            return jnp.where(even, far[at], near[at])
        if layer >= DEPTH:
            at = (field, 2 * (layer - DEPTH) + block_y, rest)
            return jnp.where(even, near[at], far[at])
        return own[field, 2 * layer + block_y, rest]

    for field in range(FIELDS):
        for pair in range(pairs):
            to = (pair % 2) * 4
            one, two = pair - 2, pair - 2 + pairs
            lower[field, pair // 2, to : to + 4, :] = jnp.where(
                first_half, rows(field, one, 0), pltpu.roll(rows(field, two, 0), 64, 1)
            )
            upper[field, pair // 2, to : to + 4, :] = jnp.where(
                first_half, pltpu.roll(rows(field, one, 1), 64, 1), rows(field, two, 1)
            )


def minmod(left, right):
    return jnp.maximum(jnp.minimum(left, right), 0.0) + jnp.minimum(jnp.maximum(left, right), 0.0)


def primitives(conserved):
    density, mx, my, mz, energy = conserved
    inverse = 1.0 / density
    vx, vy, vz = mx * inverse, my * inverse, mz * inverse
    pressure = (GAMMA - 1.0) * (energy - 0.5 * (mx * vx + my * vy + mz * vz))
    return [density, vx, vy, vz, pressure]


def face_terms(primitive, normal):
    density, vx, vy, vz, pressure = primitive
    energy = pressure * (1.0 / (GAMMA - 1.0)) + (0.5 * density) * (vx * vx + vy * vy + vz * vz)
    conserved = [density, density * vx, density * vy, density * vz, energy]
    stiff = GAMMA * pressure
    sound = stiff * lax.rsqrt(stiff * density)
    return conserved, primitive[1 + normal], pressure, sound


def face_flux(left, right, normal):
    left_u, left_v, left_p, left_c = face_terms(left, normal)
    right_u, right_v, right_p, right_c = face_terms(right, normal)
    fastest = jnp.maximum(jnp.maximum(left_v + left_c, right_v + right_c), 0.0)
    slowest = jnp.minimum(jnp.minimum(left_v - left_c, right_v - right_c), 0.0)
    inverse = 1.0 / (fastest - slowest)
    plus = fastest * inverse
    minus = slowest * inverse
    left_weight = plus * (left_v - slowest)
    right_weight = minus * (right_v - fastest)
    left_push = plus * left_p
    right_push = minus * right_p
    fluxes = [left_weight * a - right_weight * b for a, b in zip(left_u, right_u)]
    fluxes[1 + normal] = fluxes[1 + normal] + (left_push - right_push)
    fluxes[4] = fluxes[4] + (left_push * left_v - right_push * right_v)
    return fluxes


def shift_x(value, amount):
    axis = value.ndim - 1
    x = lax.broadcasted_iota(jnp.int32, value.shape, axis) % 16
    if amount > 0:
        inner = pltpu.roll(value, 1, axis)
        outer = pltpu.roll(pltpu.roll(value, 2, axis - 1), LANES - 15, axis)
        return jnp.where(x == 0, outer, inner)
    inner = pltpu.roll(value, LANES - 1, axis)
    outer = pltpu.roll(pltpu.roll(value, ROWS - 2, axis - 1), 15, axis)
    return jnp.where(x == 15, outer, inner)


def shift_y(value, amount):
    shape = value[0].shape
    across, down = len(shape) - 1, len(shape) - 2
    lane = lax.broadcasted_iota(jnp.int32, shape, across)
    odd = lax.broadcasted_iota(jnp.int32, shape, down) % 2 == 1
    if amount > 0:
        moved = [pltpu.roll(v, 16, across) for v in value]
        upper = moved
        lower = [moved[i - 1] for i in range(3)]
        outer = lane < 16
    else:
        moved = [pltpu.roll(v, LANES - 16, across) for v in value]
        upper = [moved[(i + 1) % 3] for i in range(3)]
        lower = moved
        outer = lane >= LANES - 16
    edge = [
        jnp.where(odd, pltpu.roll(u, 1, down), pltpu.roll(l, ROWS - 1, down))
        for u, l in zip(upper, lower)
    ]
    return [jnp.where(outer, e, m) for e, m in zip(edge, moved)]


def sweep_x(primitive):
    ahead = [shift_x(q, -1) for q in primitive]
    steps = [b - q for q, b in zip(primitive, ahead)]
    half = [0.5 * minmod(shift_x(d, 1), d) for d in steps]
    left = [q + h for q, h in zip(primitive, half)]
    right = [shift_x(q - h, -1) for q, h in zip(primitive, half)]
    return [shift_x(f, 1) - f for f in face_flux(left, right, 0)]


def sweep_y(primitive):
    left, right = [], []
    for q in primitive:
        ahead = shift_y(q, -1)
        steps = [b - a for a, b in zip(q, ahead)]
        behind = shift_y(steps, 1)
        half = [0.5 * minmod(b, d) for b, d in zip(behind, steps)]
        left.append([a + h for a, h in zip(q, half)])
        right.append(shift_y([a - h for a, h in zip(q, half)], -1))
    fluxes = [face_flux([l[i] for l in left], [r[i] for r in right], 1) for i in range(3)]
    out = []
    for field in range(FIELDS):
        flux = [fluxes[i][field] for i in range(3)]
        out.append([b - f for b, f in zip(shift_y(flux, 1), flux)])
    return out


BATCH = 4


def rate_x(total, prim, target, source, count, blocks, batch=BATCH):
    def planes(step, carry):
        z = step * batch
        values = [prim[f, pl.ds(z + source, batch), blocks] for f in range(FIELDS)]
        for f, change in enumerate(sweep_x(values)):
            total[f, pl.ds(z + target, batch), blocks] = change
        return carry

    lax.fori_loop(0, count // batch, planes, 0)


def rate_z(total, prim, count, blocks):
    def load(z):
        return [prim[f, z, blocks] for f in range(FIELDS)]

    here, ahead = load(1), load(2)
    step = [h - b for h, b in zip(here, load(0))]
    ahead_step = [a - h for a, h in zip(ahead, here)]
    half = [0.5 * minmod(a, b) for a, b in zip(step, ahead_step)]

    def face(z, here, half, ahead, ahead_step):
        beyond = load(z + 3)
        beyond_step = [b - a for a, b in zip(ahead, beyond)]
        ahead_half = [0.5 * minmod(a, b) for a, b in zip(ahead_step, beyond_step)]
        left = [q + h for q, h in zip(here, half)]
        right = [q - h for q, h in zip(ahead, ahead_half)]
        return ahead, ahead_half, beyond, beyond_step, face_flux(left, right, 2)

    def layer(z, state):
        after = face(z + 1, *state[:4])
        for f in range(FIELDS):
            total[f, z, blocks] = total[f, z, blocks] + (state[4][f] - after[4][f])
        return after

    lax.fori_loop(0, count, layer, face(0, here, half, ahead, ahead_step))


INNER = slice(0, 2)
EDGE = slice(2, 3)


def inner_kernel(near, far, prim, x_change, w0, change):
    for z in range(HALO):
        index = (slice(None), slice(2 * z, 2 * z + 2))
        below, above = below_above(near, far, index)
        for base, piece in ((0, below), (HALO + DEPTH, above)):
            values = [piece[f] for f in range(FIELDS)]
            for f, value in enumerate(primitives(values)):
                w0[f, base + z] = value
    for f in range(FIELDS):
        w0[f, HALO : HALO + DEPTH] = prim[f]
        change[f, 2 : 2 + DEPTH] = x_change[f]
    rate_x(change, w0, 0, 2, 2, INNER, 2)
    rate_x(change, w0, 2 + DEPTH, HALO + DEPTH, 2, INNER, 2)
    rate_z(change, w0, WIDE, INNER)


def rate_y(prims, store, count):
    def planes(step, carry):
        here = pl.ds(step * BATCH, BATCH)
        shifted = pl.ds(step * BATCH + 2, BATCH)
        store(here, sweep_y(prims(here, shifted)))
        return carry

    lax.fori_loop(0, count // BATCH, planes, 0)


def advance_kernel(
    counts, near, far, own, w0, inner, from_above, from_below, state,
    uh, wh, changeh, total, u1, w1, change, final,
):
    first_half = lax.broadcasted_iota(jnp.int32, (4, LANES), 1) < 64
    pairs = WIDE // 2
    for field in range(FIELDS):
        for pair in range(pairs):
            rows = slice((pair % 2) * 4, (pair % 2) * 4 + 4)
            above = from_above[field, pair // 2, rows, :]
            below = from_below[field, pair // 2, rows, :]
            for z, halo in (
                (pair, jnp.where(first_half, above, pltpu.roll(below, 64, 1))),
                (pair + pairs, jnp.where(first_half, pltpu.roll(above, 64, 1), below)),
            ):
                uh[field, z, 0, pl.ds(0, 4, stride=2), :] = halo
                uh[field, z, 0, pl.ds(1, 4, stride=2), :] = halo

    def halo_primitive(step, carry):
        layers = pl.ds(step * BATCH, BATCH)
        values = [uh[f, layers] for f in range(FIELDS)]
        for f, value in enumerate(primitives(values)):
            wh[f, layers] = value
        return carry

    lax.fori_loop(0, WIDE // BATCH, halo_primitive, 0)

    rate_x(changeh, wh, 0, 2, DEPTH, slice(0, 1), 2 * BATCH)
    rate_z(changeh, wh, DEPTH, slice(0, 1))

    def first_prims(here, shifted):
        return [[w0[f, shifted, 0], w0[f, shifted, 1], wh[f, here, 0]] for f in range(FIELDS)]

    def first_store(here, changes):
        for f in range(FIELDS):
            for i in range(2):
                total[f, here, i] = inner[f, here, i] + changes[f][i]
            total[f, here, 2] = changes[f][2]

    rate_y(first_prims, first_store, WIDE)

    def first_step(base, layer):
        values = [v + TIME_STEP * total[f, layer, INNER] for f, v in enumerate(base)]
        for f, value in enumerate(values):
            u1[f, layer] = value
        for f, value in enumerate(primitives(values)):
            w1[f, layer, INNER] = value

    for z in range(2):
        below, _ = below_above(near, far, (slice(None), slice(2 * z + 4, 2 * z + 6)))
        _, above = below_above(near, far, (slice(None), slice(2 * z, 2 * z + 2)))
        first_step([below[f] for f in range(FIELDS)], z)
        first_step([above[f] for f in range(FIELDS)], z + 2 + DEPTH)

    def own_step(step, carry):
        for k in range(2):
            z = 2 * step + k
            first_step([own[f, pl.ds(2 * z, 2)] for f in range(FIELDS)], z + 2)
        layers, shifted = pl.ds(2 * step, 2), pl.ds(2 * step + 2, 2)
        values = [
            uh[f, shifted] + TIME_STEP * (total[f, shifted, EDGE] + changeh[f, layers])
            for f in range(FIELDS)
        ]
        for f, value in enumerate(primitives(values)):
            w1[f, shifted, EDGE] = value
        return carry

    lax.fori_loop(0, DEPTH // 2, own_step, 0)

    rate_x(change, w1, 0, 2, DEPTH, INNER)
    rate_z(change, w1, DEPTH, INNER)

    def last_prims(here, shifted):
        return [[w1[f, shifted, i] for i in range(3)] for f in range(FIELDS)]

    def last_store(here, changes):
        after = pl.ds(here.start + 2, BATCH)
        for f in range(FIELDS):
            for i in range(2):
                u0 = jnp.stack([own[f, 2 * (here.start + k) + i] for k in range(BATCH)])
                rate = change[f, here, i] + changes[f][i]
                final[f, here, i] = 0.5 * u0 + 0.5 * (u1[f, after, i] + TIME_STEP * rate)

    rate_y(last_prims, last_store, DEPTH)

    position = lax.axis_index("blk") % GROUP
    start = jnp.int32(0)
    count = jnp.int32(0)
    for device in range(GROUP):
        start = start + jnp.where(device < position, counts[device], 0)
        count = jnp.where(device == position, counts[device], count)
    for slot in range(SLOTS):
        key = jnp.minimum(start + slot, KEYS - 1)
        block_y, xb = key // 4, key % 4
        valid = slot < count
        for field in range(FIELDS):
            for z in range(DEPTH):
                block = final[field, z, block_y, pl.ds(2 * xb, 2), :]
                state[field, pl.ds(8 * z + slot, 2, stride=SLOTS), :] = jnp.where(
                    valid, block, 0.0
                )


def body(state_old, counts_old, counts_new):
    slabs = lax.axis_size("gz")
    places = lax.axis_size("blk")
    groups = places // GROUP
    slab = lax.axis_index("gz")
    place = lax.axis_index("blk")
    group = place // GROUP

    def row_of(counts):
        return lax.dynamic_slice(counts, (slab, group, 0), (1, 1, GROUP)).reshape(GROUP)

    old_here = row_of(counts_old)
    new_here = row_of(counts_new)
    members = [[g * GROUP + k for k in range(GROUP)] for g in range(groups)]

    def along_y(value, by):
        route = [(i, (i + by * GROUP) % places) for i in range(places)]
        return lax.ppermute(value, "blk", route)

    def trade(value, offset):
        route = []
        for g in range(slabs):
            partner = ((g + offset) ^ 1) - offset
            for i in range(places):
                route.append((g * places + i, partner % slabs * places + i))
        return lax.ppermute(value, ("gz", "blk"), route)

    lines = DEPTH * 2
    held = state_old.reshape(SLOTS, FIELDS, lines, LANES).transpose(1, 2, 0, 3)
    held = held.reshape(FIELDS, lines * SLOTS, LANES)
    received = lax.all_gather(held, "blk", axis_index_groups=members)

    layers = f32(FIELDS, 2 * HALO, ROWS, LANES)
    to_near, to_far = call(outer_kernel, [layers, layers], [SMEM, VMEM])(old_here, received)
    near = trade(to_near, 0)
    far = trade(to_far, 1)
    block = f32(FIELDS, DEPTH, 2, ROWS, LANES)
    own, prim, x_change = call(
        own_kernel,
        [f32(FIELDS, 2 * DEPTH, ROWS, LANES), block, block],
        [SMEM, VMEM],
        flops=1 << 24,
    )(old_here, received)

    edge = f32(FIELDS, WIDE // 4, ROWS, LANES)
    lower, upper = call(edge_kernel, [edge, edge], [VMEM] * 3)(near, far, own)
    from_above = along_y(lower, -1)
    from_below = along_y(upper, 1)
    w0, inner = call(
        inner_kernel,
        [f32(FIELDS, DEEP, 2, ROWS, LANES), f32(FIELDS, WIDE, 2, ROWS, LANES)],
        [VMEM] * 4,
        flops=1 << 24,
    )(near, far, prim, x_change)

    def work(*shape):
        return pltpu.VMEM((FIELDS,) + shape + (ROWS, LANES), jnp.float32)

    state = call(
        advance_kernel,
        f32(FIELDS, lines * SLOTS, LANES),
        [SMEM] + [VMEM] * 7,
        [work(WIDE, 1), work(WIDE, 1), work(DEPTH, 1), work(WIDE, 3)]
        + [work(WIDE, 2), work(WIDE, 3), work(DEPTH, 2), work(DEPTH, 2)],
        flops=1 << 24,
    )(new_here, near, far, own, w0, inner, from_above, from_below)
    state = state.reshape(FIELDS, lines, SLOTS, LANES).transpose(2, 0, 1, 3)
    return state.reshape(1, 1, SLOTS, FIELDS, lines * LANES)


def solution(mesh):
    in_specs = (P("gz", "blk", None, None, None), P(), P())
    out_specs = P("gz", "blk", None, None, None)
    return jax.shard_map(body, mesh=mesh, in_specs=in_specs, out_specs=out_specs, check_vma=False)
```

```python
import jax
import jax.numpy as jnp
from jax import lax
from jax.experimental import pallas as pl
from jax.experimental.pallas import tpu as pltpu
from jax.sharding import PartitionSpec as P


FIELDS = 5
GROUP = 4
SLOTS = 4
KEYS = 8
ROWS = 8
LANES = 128
QUARTER = 4
HALO = 4
LINES = ROWS * SLOTS

TIME_STEP = 0.08
GAMMA = 1.4

VMEM = pl.BlockSpec(memory_space=pltpu.VMEM)
SMEM = pl.BlockSpec(memory_space=pltpu.SMEM)
HBM = pl.BlockSpec(memory_space=pltpu.HBM)


def call(kernel, out_shapes, in_specs, scratch=(), flops=0, out=VMEM):
    return pl.pallas_call(
        kernel,
        out_shape=out_shapes,
        in_specs=in_specs,
        out_specs=jax.tree.map(lambda _: out, out_shapes),
        scratch_shapes=list(scratch),
        compiler_params=pltpu.CompilerParams(vmem_limit_bytes=24 << 20),
        cost_estimate=pl.CostEstimate(flops=flops, bytes_accessed=1 << 20, transcendentals=0),
    )


def f32(*shape):
    return jax.ShapeDtypeStruct(shape, jnp.float32)


def quarter_of(device):
    return jnp.where(lax.axis_index("gz") % 2 == 0, device, GROUP - 1 - device)


def even_quarter():
    return (lax.axis_index("blk") + lax.axis_index("gz")) % 2 == 0


def split_kernel(state, message, arrived):
    copies = []
    for device in range(GROUP):
        rows = pl.ds(pl.multiple_of(quarter_of(device) * LINES, LINES), LINES)
        copies.append(
            pltpu.make_async_copy(state.at[:, rows], message.at[device], arrived.at[device])
        )
    for copy in copies:
        copy.start()
    for copy in copies:
        copy.wait()


def join_kernel(received, state, arrived):
    copies = []
    for device in range(GROUP):
        rows = pl.ds(pl.multiple_of(quarter_of(device) * LINES, LINES), LINES)
        copies.append(
            pltpu.make_async_copy(received.at[device], state.at[:, rows], arrived.at[device])
        )
    for copy in copies:
        copy.start()
    for copy in copies:
        copy.wait()


def place_of(counts, key):
    position = jnp.int32(0)
    first = jnp.int32(0)
    upto = jnp.int32(0)
    for device in range(GROUP - 1):
        upto = upto + counts[device]
        beyond = upto <= key
        position = position + beyond.astype(jnp.int32)
        first = jnp.where(beyond, upto, first)
    return position, jnp.clip(key - first, 0, SLOTS - 1)


def gather_kernel(counts, received, piece):
    for block_y in range(2):
        for xb in range(4):
            device, slot = place_of(counts, block_y * 4 + xb)
            for field in range(FIELDS):
                block = received[device, field, pl.ds(slot, ROWS, stride=SLOTS), :]
                for z in range(QUARTER):
                    piece[field, z * 2 + block_y, 2 * xb : 2 * xb + 2, :] = block[
                        2 * z : 2 * z + 2
                    ]


def below_above(first, second, index):
    even = even_quarter()
    return (
        jnp.where(even, second[index], first[index]),
        jnp.where(even, first[index], second[index]),
    )


def edge_kernel(first, own, second, lower, upper):
    first_half = lax.broadcasted_iota(jnp.int32, (4, LANES), 1) < 64

    def rows(field, layer, block_y):
        rest = pl.ds(block_y, 4, stride=2)
        if layer < 0:
            return below_above(first, second, (field, 2 * (layer + HALO) + block_y, rest))[0]
        if layer >= QUARTER:
            return below_above(first, second, (field, 2 * (layer - QUARTER) + block_y, rest))[1]
        return own[field, 2 * layer + block_y, rest]

    for field in range(FIELDS):
        for pair in range(4):
            to = (pair % 2) * 4
            one, two = pair - 2, pair + 2
            lower[field, pair // 2, to : to + 4, :] = jnp.where(
                first_half, rows(field, one, 0), pltpu.roll(rows(field, two, 0), 64, 1)
            )
            upper[field, pair // 2, to : to + 4, :] = jnp.where(
                first_half, pltpu.roll(rows(field, one, 1), 64, 1), rows(field, two, 1)
            )


def minmod(left, right):
    return jnp.maximum(jnp.minimum(left, right), 0.0) + jnp.minimum(jnp.maximum(left, right), 0.0)


def primitives(conserved):
    density, mx, my, mz, energy = conserved
    inverse = 1.0 / density
    vx, vy, vz = mx * inverse, my * inverse, mz * inverse
    pressure = (GAMMA - 1.0) * (energy - 0.5 * (mx * vx + my * vy + mz * vz))
    return [density, vx, vy, vz, pressure]


def face_terms(primitive, normal):
    density, vx, vy, vz, pressure = primitive
    energy = pressure * (1.0 / (GAMMA - 1.0)) + (0.5 * density) * (vx * vx + vy * vy + vz * vz)
    conserved = [density, density * vx, density * vy, density * vz, energy]
    stiff = GAMMA * pressure
    sound = stiff * lax.rsqrt(stiff * density)
    return conserved, primitive[1 + normal], pressure, sound


def face_flux(left, right, normal):
    left_u, left_v, left_p, left_c = face_terms(left, normal)
    right_u, right_v, right_p, right_c = face_terms(right, normal)
    fastest = jnp.maximum(jnp.maximum(left_v + left_c, right_v + right_c), 0.0)
    slowest = jnp.minimum(jnp.minimum(left_v - left_c, right_v - right_c), 0.0)
    inverse = 1.0 / (fastest - slowest)
    plus = fastest * inverse
    minus = slowest * inverse
    left_weight = plus * (left_v - slowest)
    right_weight = minus * (right_v - fastest)
    left_push = plus * left_p
    right_push = minus * right_p
    fluxes = [left_weight * a - right_weight * b for a, b in zip(left_u, right_u)]
    fluxes[1 + normal] = fluxes[1 + normal] + (left_push - right_push)
    fluxes[4] = fluxes[4] + (left_push * left_v - right_push * right_v)
    return fluxes


def shift_x(value, amount):
    axis = value.ndim - 1
    x = lax.broadcasted_iota(jnp.int32, value.shape, axis) % 16
    if amount > 0:
        inner = pltpu.roll(value, 1, axis)
        outer = pltpu.roll(pltpu.roll(value, 2, axis - 1), LANES - 15, axis)
        return jnp.where(x == 0, outer, inner)
    inner = pltpu.roll(value, LANES - 1, axis)
    outer = pltpu.roll(pltpu.roll(value, ROWS - 2, axis - 1), 15, axis)
    return jnp.where(x == 15, outer, inner)


def shift_y(value, amount):
    shape = value[0].shape
    across, down = len(shape) - 1, len(shape) - 2
    lane = lax.broadcasted_iota(jnp.int32, shape, across)
    odd = lax.broadcasted_iota(jnp.int32, shape, down) % 2 == 1
    if amount > 0:
        moved = [pltpu.roll(v, 16, across) for v in value]
        upper = moved
        lower = [moved[i - 1] for i in range(3)]
        outer = lane < 16
    else:
        moved = [pltpu.roll(v, LANES - 16, across) for v in value]
        upper = [moved[(i + 1) % 3] for i in range(3)]
        lower = moved
        outer = lane >= LANES - 16
    edge = [
        jnp.where(odd, pltpu.roll(u, 1, down), pltpu.roll(l, ROWS - 1, down))
        for u, l in zip(upper, lower)
    ]
    return [jnp.where(outer, e, m) for e, m in zip(edge, moved)]


def sweep_x(primitive):
    ahead = [shift_x(q, -1) for q in primitive]
    steps = [b - q for q, b in zip(primitive, ahead)]
    half = [0.5 * minmod(shift_x(d, 1), d) for d in steps]
    left = [q + h for q, h in zip(primitive, half)]
    right = [shift_x(q - h, -1) for q, h in zip(primitive, half)]
    return [shift_x(f, 1) - f for f in face_flux(left, right, 0)]


def sweep_y(primitive):
    ahead = [shift_y(q, -1) for q in primitive]
    steps = [[b - a for a, b in zip(q, after)] for q, after in zip(primitive, ahead)]
    behind = [shift_y(d, 1) for d in steps]
    half = [[0.5 * minmod(a, b) for a, b in zip(p, d)] for p, d in zip(behind, steps)]
    beyond = [shift_y(h, -1) for h in half]
    fluxes = []
    for i in range(3):
        left = [q[i] + h[i] for q, h in zip(primitive, half)]
        right = [q[i] - h[i] for q, h in zip(ahead, beyond)]
        fluxes.append(face_flux(left, right, 1))
    out = []
    for flux in zip(*fluxes):
        out.append([b - f for b, f in zip(shift_y(list(flux), 1), flux)])
    return out


X_LAYERS = 4
Y_LAYERS = 4


def rate_x(total, prim, count, blocks):
    def planes(step, carry):
        z = step * X_LAYERS
        values = [prim[f, pl.ds(z + 2, X_LAYERS), blocks] for f in range(FIELDS)]
        for f, change in enumerate(sweep_x(values)):
            total[f, pl.ds(z, X_LAYERS), blocks] = change
        return carry

    lax.fori_loop(0, count // X_LAYERS, planes, 0)


def rate_z(total, prim, count, blocks):
    def load(z):
        return [prim[f, z, blocks] for f in range(FIELDS)]

    here, ahead = load(1), load(2)
    step = [h - b for h, b in zip(here, load(0))]
    ahead_step = [a - h for a, h in zip(ahead, here)]
    half = [0.5 * minmod(a, b) for a, b in zip(step, ahead_step)]

    def face(z, here, half, ahead, ahead_step):
        beyond = load(z + 3)
        beyond_step = [b - a for a, b in zip(ahead, beyond)]
        ahead_half = [0.5 * minmod(a, b) for a, b in zip(ahead_step, beyond_step)]
        left = [q + h for q, h in zip(here, half)]
        right = [q - h for q, h in zip(ahead, ahead_half)]
        return ahead, ahead_half, beyond, beyond_step, face_flux(left, right, 2)

    def layer(z, state):
        after = face(z + 1, *state[:4])
        for f in range(FIELDS):
            total[f, z, blocks] = total[f, z, blocks] + (state[4][f] - after[4][f])
        return after

    lax.fori_loop(0, count, layer, face(0, here, half, ahead, ahead_step))


INNER = slice(0, 2)
EDGE = slice(2, 3)


def inner_kernel(first, own, second, w0, change):
    for z in range(QUARTER):
        index = (slice(None), slice(2 * z, 2 * z + 2))
        below, above = below_above(first, second, index)
        for base, piece in ((0, below), (QUARTER, own[index]), (2 * QUARTER, above)):
            values = [piece[f] for f in range(FIELDS)]
            for f, value in enumerate(primitives(values)):
                w0[f, base + z] = value
    rate_x(change, w0, QUARTER + HALO, INNER)
    rate_z(change, w0, QUARTER + HALO, INNER)


def first_step(layer, base, u1, w1, total):
    values = [base[f] + TIME_STEP * total[f, layer, INNER] for f in range(FIELDS)]
    for f, value in enumerate(values):
        u1[f, layer] = value
    for f, value in enumerate(primitives(values)):
        w1[f, layer, INNER] = value


def advance_kernel(
    counts, first, own, second, w0, inner, from_above, from_below, message,
    uh, wh, changeh, total, u1, w1, change, done,
):
    wide = QUARTER + HALO
    first_half = lax.broadcasted_iota(jnp.int32, (4, LANES), 1) < 64
    for field in range(FIELDS):
        for pair in range(4):
            rows = slice((pair % 2) * 4, (pair % 2) * 4 + 4)
            above = from_above[field, pair // 2, rows, :]
            below = from_below[field, pair // 2, rows, :]
            for z, halo in (
                (pair, jnp.where(first_half, above, pltpu.roll(below, 64, 1))),
                (pair + 4, jnp.where(first_half, pltpu.roll(above, 64, 1), below)),
            ):
                uh[field, z, 0, pl.ds(0, 4, stride=2), :] = halo
                uh[field, z, 0, pl.ds(1, 4, stride=2), :] = halo
    for f, value in enumerate(primitives([uh[f] for f in range(FIELDS)])):
        wh[f] = value

    rate_x(changeh, wh, QUARTER, slice(0, 1))
    rate_z(changeh, wh, QUARTER, slice(0, 1))

    def planes(step, carry):
        z = step * Y_LAYERS
        here, shifted = pl.ds(z, Y_LAYERS), pl.ds(z + 2, Y_LAYERS)
        prims = [[w0[f, shifted, 0], w0[f, shifted, 1], wh[f, here, 0]] for f in range(FIELDS)]
        changes = sweep_y(prims)
        for f in range(FIELDS):
            for i in range(2):
                total[f, here, i] = inner[f, here, i] + changes[f][i]
            total[f, here, 2] = changes[f][2]
        return carry

    lax.fori_loop(0, wide // Y_LAYERS, planes, 0)

    for z in range(QUARTER):
        index = (slice(None), slice(2 * z, 2 * z + 2))
        if z >= 2:
            layer, piece = z - 2, below_above(first, second, index)[0]
            first_step(layer, piece, u1, w1, total)
        else:
            layer, piece = z + 2 + QUARTER, below_above(first, second, index)[1]
            first_step(layer, piece, u1, w1, total)
        first_step(z + 2, own[index], u1, w1, total)
    for z in range(QUARTER):
        values = [
            uh[f, z + 2] + TIME_STEP * (total[f, z + 2, EDGE] + changeh[f, z])
            for f in range(FIELDS)
        ]
        for f, value in enumerate(primitives(values)):
            w1[f, z + 2, EDGE] = value

    rate_x(change, w1, QUARTER, INNER)
    rate_z(change, w1, QUARTER, INNER)

    def last_planes(step, carry):
        z = step * 4
        here, shifted = pl.ds(z, 4), pl.ds(z + 2, 4)
        changes = sweep_y([[w1[f, shifted, i] for i in range(3)] for f in range(FIELDS)])
        for f in range(FIELDS):
            for i in range(2):
                change[f, here, i] = change[f, here, i] + changes[f][i]
        return carry

    lax.fori_loop(0, 1, last_planes, 0)

    for z in range(QUARTER):
        for field in range(FIELDS):
            for block_y in range(2):
                value = 0.5 * own[field, 2 * z + block_y] + 0.5 * (
                    u1[field, z + 2, block_y] + TIME_STEP * change[field, z, block_y]
                )
                for xb in range(4):
                    done[block_y * 4 + xb, field, 2 * z : 2 * z + 2, :] = value[
                        2 * xb : 2 * xb + 2, :
                    ]

    start = jnp.int32(0)
    for device in range(GROUP):
        for slot in range(SLOTS):
            key = jnp.minimum(start + slot, KEYS - 1)
            valid = slot < counts[device]
            for field in range(FIELDS):
                message[device, field, pl.ds(slot, ROWS, stride=SLOTS), :] = jnp.where(
                    valid, done[key, field], 0.0
                )
        start = start + counts[device]


def body(state_old, counts_old, counts_new):
    slabs = lax.axis_size("gz")
    places = lax.axis_size("blk")
    groups = places // GROUP
    slab = lax.axis_index("gz")
    group = lax.axis_index("blk") // GROUP

    def row_of(counts):
        return lax.dynamic_slice(counts, (slab, group, 0), (1, 1, GROUP)).reshape(GROUP)

    old_here = row_of(counts_old)
    new_here = row_of(counts_new)
    members = [[g * GROUP + k for k in range(GROUP)] for g in range(groups)]

    def exchange(message):
        return lax.all_to_all(message, "blk", 0, 0, axis_index_groups=members)

    def along_y(value, by):
        route = [(i, (i + by * GROUP) % places) for i in range(places)]
        return lax.ppermute(value, "blk", route)

    def trade(value, offset):
        def device_of(quarter):
            g, k = divmod(quarter, GROUP)
            return g, k if g % 2 == 0 else GROUP - 1 - k

        route = []
        for quarter in range(slabs * GROUP):
            partner = (((quarter + offset) ^ 1) - offset) % (slabs * GROUP)
            (g, j), (to_g, to_j) = device_of(quarter), device_of(partner)
            for i in range(0, places, GROUP):
                route.append((g * places + i + j, to_g * places + i + to_j))
        return lax.ppermute(value, ("gz", "blk"), route)

    parts = f32(GROUP, FIELDS, LINES, LANES)
    slots = f32(FIELDS, GROUP * LINES, LANES)
    wide = QUARTER + HALO
    held = state_old.reshape(SLOTS, FIELDS, GROUP * ROWS, LANES).transpose(1, 2, 0, 3)
    held = held.reshape(slots.shape)
    arrivals = [pltpu.SemaphoreType.DMA((GROUP,))]
    received = exchange(call(split_kernel, parts, [HBM], arrivals)(held))

    own = call(gather_kernel, f32(FIELDS, 2 * QUARTER, ROWS, LANES), [SMEM, VMEM])(
        old_here, received
    )
    first = trade(own, 0)
    second = trade(own, 1)

    edge = f32(FIELDS, 2, ROWS, LANES)
    lower, upper = call(edge_kernel, [edge, edge], [VMEM] * 3)(first, own, second)
    from_above = along_y(lower, -1)
    from_below = along_y(upper, 1)
    w0, inner = call(
        inner_kernel,
        [f32(FIELDS, wide + HALO, 2, ROWS, LANES), f32(FIELDS, wide, 2, ROWS, LANES)],
        [VMEM] * 3,
        flops=1 << 24,
    )(first, own, second)

    def work(*shape):
        return pltpu.VMEM((FIELDS,) + shape + (ROWS, LANES), jnp.float32)

    finished = call(
        advance_kernel,
        parts,
        [SMEM] + [VMEM] * 7,
        [work(wide, 1), work(wide, 1), work(QUARTER, 1), work(wide, 3)]
        + [work(wide, 2), work(wide, 3), work(QUARTER, 2)]
        + [pltpu.VMEM((KEYS, FIELDS, ROWS, LANES), jnp.float32)],
        flops=1 << 24,
    )(new_here, first, own, second, w0, inner, from_above, from_below)
    returned = exchange(finished)
    state = call(join_kernel, slots, [VMEM], arrivals, out=HBM)(returned)
    state = state.reshape(FIELDS, GROUP * ROWS, SLOTS, LANES).transpose(2, 0, 1, 3)
    return state.reshape(state_old.shape)


def solution(mesh):
    in_specs = (P("gz", "blk", None, None, None), P(), P())
    out_specs = P("gz", "blk", None, None, None)
    return jax.shard_map(body, mesh=mesh, in_specs=in_specs, out_specs=out_specs, check_vma=False)
```

```python
import jax
import jax.numpy as jnp
from jax import lax
from jax.experimental import pallas as pl
from jax.experimental.pallas import tpu as pltpu
from jax.sharding import PartitionSpec as P


FIELDS = 5
GROUP = 4
SLOTS = 4
KEYS = 8
ROWS = 8
LANES = 128
QUARTER = 4
HALO = 4
LINES = ROWS * SLOTS

TIME_STEP = 0.08
GAMMA = 1.4

VMEM = pl.BlockSpec(memory_space=pltpu.VMEM)
HBM = pl.BlockSpec(memory_space=pl.ANY)


def call(kernel, out_shapes, in_specs, scratch=(), flops=0, out=VMEM):
    return pl.pallas_call(
        kernel,
        out_shape=out_shapes,
        in_specs=in_specs,
        out_specs=jax.tree.map(lambda _: out, out_shapes),
        scratch_shapes=list(scratch),
        compiler_params=pltpu.CompilerParams(vmem_limit_bytes=24 << 20),
        cost_estimate=pl.CostEstimate(flops=flops, bytes_accessed=1 << 20, transcendentals=0),
    )


def f32(*shape):
    return jax.ShapeDtypeStruct(shape, jnp.float32)


def quarter_of(device):
    return jnp.where(lax.axis_index("gz") % 2 == 0, device, GROUP - 1 - device)


def even_quarter():
    return (lax.axis_index("blk") + lax.axis_index("gz")) % 2 == 0


def split_kernel(state, message):
    for device in range(GROUP):
        rows = pl.ds(pl.multiple_of(quarter_of(device) * LINES, LINES), LINES)
        message[device] = state[:, rows]


def join_kernel(received, state, arrived):
    copies = []
    for device in range(GROUP):
        rows = pl.ds(pl.multiple_of(quarter_of(device) * LINES, LINES), LINES)
        copies.append(
            pltpu.make_async_copy(received.at[device], state.at[:, rows], arrived.at[device])
        )
    for copy in copies:
        copy.start()
    for copy in copies:
        copy.wait()


def place_of(counts, key):
    position = jnp.int32(0)
    first = jnp.int32(0)
    upto = jnp.int32(0)
    for device in range(GROUP - 1):
        upto = upto + counts[device]
        beyond = upto <= key
        position = position + beyond.astype(jnp.int32)
        first = jnp.where(beyond, upto, first)
    return position, jnp.clip(key - first, 0, SLOTS - 1)


def gather_kernel(held_counts, received, piece):
    row = held_counts[...]
    counts = [row[0, device] for device in range(GROUP)]
    for block_y in range(2):
        for xb in range(4):
            device, slot = place_of(counts, block_y * 4 + xb)
            for field in range(FIELDS):
                block = received[device, field, pl.ds(slot, ROWS, stride=SLOTS), :]
                for z in range(QUARTER):
                    piece[field, z * 2 + block_y, 2 * xb : 2 * xb + 2, :] = block[
                        2 * z : 2 * z + 2
                    ]


def below_above(first, second, index):
    even = even_quarter()
    return (
        jnp.where(even, second[index], first[index]),
        jnp.where(even, first[index], second[index]),
    )


def edge_kernel(first, own, second, lower, upper):
    first_half = lax.broadcasted_iota(jnp.int32, (4, LANES), 1) < 64

    def rows(field, layer, block_y):
        rest = pl.ds(block_y, 4, stride=2)
        if layer < 0:
            return below_above(first, second, (field, 2 * (layer + HALO) + block_y, rest))[0]
        if layer >= QUARTER:
            return below_above(first, second, (field, 2 * (layer - QUARTER) + block_y, rest))[1]
        return own[field, 2 * layer + block_y, rest]

    for field in range(FIELDS):
        for pair in range(4):
            to = (pair % 2) * 4
            one, two = pair - 2, pair + 2
            lower[field, pair // 2, to : to + 4, :] = jnp.where(
                first_half, rows(field, one, 0), pltpu.roll(rows(field, two, 0), 64, 1)
            )
            upper[field, pair // 2, to : to + 4, :] = jnp.where(
                first_half, pltpu.roll(rows(field, one, 1), 64, 1), rows(field, two, 1)
            )


def minmod(left, right):
    return jnp.maximum(jnp.minimum(left, right), 0.0) + jnp.minimum(jnp.maximum(left, right), 0.0)


def primitives(conserved):
    density, mx, my, mz, energy = conserved
    inverse = 1.0 / density
    vx, vy, vz = mx * inverse, my * inverse, mz * inverse
    pressure = (GAMMA - 1.0) * (energy - 0.5 * (mx * vx + my * vy + mz * vz))
    return [density, vx, vy, vz, pressure]


def face_terms(primitive, normal):
    density, vx, vy, vz, pressure = primitive
    energy = pressure * (1.0 / (GAMMA - 1.0)) + (0.5 * density) * (vx * vx + vy * vy + vz * vz)
    conserved = [density, density * vx, density * vy, density * vz, energy]
    stiff = GAMMA * pressure
    sound = stiff * lax.rsqrt(stiff * density)
    return conserved, primitive[1 + normal], pressure, sound


def face_flux(left, right, normal):
    left_u, left_v, left_p, left_c = face_terms(left, normal)
    right_u, right_v, right_p, right_c = face_terms(right, normal)
    fastest = jnp.maximum(jnp.maximum(left_v + left_c, right_v + right_c), 0.0)
    slowest = jnp.minimum(jnp.minimum(left_v - left_c, right_v - right_c), 0.0)
    inverse = 1.0 / (fastest - slowest)
    plus = fastest * inverse
    minus = slowest * inverse
    left_weight = plus * (left_v - slowest)
    right_weight = minus * (right_v - fastest)
    left_push = plus * left_p
    right_push = minus * right_p
    fluxes = [left_weight * a - right_weight * b for a, b in zip(left_u, right_u)]
    fluxes[1 + normal] = fluxes[1 + normal] + (left_push - right_push)
    fluxes[4] = fluxes[4] + (left_push * left_v - right_push * right_v)
    return fluxes


def shift_x(value, amount):
    axis = value.ndim - 1
    x = lax.broadcasted_iota(jnp.int32, value.shape, axis) % 16
    if amount > 0:
        inner = pltpu.roll(value, 1, axis)
        outer = pltpu.roll(pltpu.roll(value, 2, axis - 1), LANES - 15, axis)
        return jnp.where(x == 0, outer, inner)
    inner = pltpu.roll(value, LANES - 1, axis)
    outer = pltpu.roll(pltpu.roll(value, ROWS - 2, axis - 1), 15, axis)
    return jnp.where(x == 15, outer, inner)


def shift_y(value, amount):
    shape = value[0].shape
    across, down = len(shape) - 1, len(shape) - 2
    lane = lax.broadcasted_iota(jnp.int32, shape, across)
    odd = lax.broadcasted_iota(jnp.int32, shape, down) % 2 == 1
    if amount > 0:
        moved = [pltpu.roll(v, 16, across) for v in value]
        upper = moved
        lower = [moved[i - 1] for i in range(3)]
        outer = lane < 16
    else:
        moved = [pltpu.roll(v, LANES - 16, across) for v in value]
        upper = [moved[(i + 1) % 3] for i in range(3)]
        lower = moved
        outer = lane >= LANES - 16
    edge = [
        jnp.where(odd, pltpu.roll(u, 1, down), pltpu.roll(l, ROWS - 1, down))
        for u, l in zip(upper, lower)
    ]
    return [jnp.where(outer, e, m) for e, m in zip(edge, moved)]


def sweep_x(primitive):
    ahead = [shift_x(q, -1) for q in primitive]
    steps = [b - q for q, b in zip(primitive, ahead)]
    half = [0.5 * minmod(shift_x(d, 1), d) for d in steps]
    left = [q + h for q, h in zip(primitive, half)]
    right = [shift_x(q - h, -1) for q, h in zip(primitive, half)]
    return [shift_x(f, 1) - f for f in face_flux(left, right, 0)]


def sweep_y(primitive):
    ahead = [shift_y(q, -1) for q in primitive]
    steps = [[b - a for a, b in zip(q, after)] for q, after in zip(primitive, ahead)]
    behind = [shift_y(d, 1) for d in steps]
    half = [[0.5 * minmod(a, b) for a, b in zip(p, d)] for p, d in zip(behind, steps)]
    beyond = [shift_y(h, -1) for h in half]
    fluxes = []
    for i in range(3):
        left = [q[i] + h[i] for q, h in zip(primitive, half)]
        right = [q[i] - h[i] for q, h in zip(ahead, beyond)]
        fluxes.append(face_flux(left, right, 1))
    out = []
    for flux in zip(*fluxes):
        out.append([b - f for b, f in zip(shift_y(list(flux), 1), flux)])
    return out


X_LAYERS = 4
Y_LAYERS = 4


def rate_x(total, prim, count, blocks):
    def planes(step, carry):
        z = step * X_LAYERS
        values = [prim[f, pl.ds(z + 2, X_LAYERS), blocks] for f in range(FIELDS)]
        for f, change in enumerate(sweep_x(values)):
            total[f, pl.ds(z, X_LAYERS), blocks] = change
        return carry

    lax.fori_loop(0, count // X_LAYERS, planes, 0)


def rate_z(total, prim, count, blocks):
    def load(z):
        return [prim[f, z, blocks] for f in range(FIELDS)]

    here, ahead = load(1), load(2)
    step = [h - b for h, b in zip(here, load(0))]
    ahead_step = [a - h for a, h in zip(ahead, here)]
    half = [0.5 * minmod(a, b) for a, b in zip(step, ahead_step)]

    def face(z, here, half, ahead, ahead_step):
        beyond = load(z + 3)
        beyond_step = [b - a for a, b in zip(ahead, beyond)]
        ahead_half = [0.5 * minmod(a, b) for a, b in zip(ahead_step, beyond_step)]
        left = [q + h for q, h in zip(here, half)]
        right = [q - h for q, h in zip(ahead, ahead_half)]
        return ahead, ahead_half, beyond, beyond_step, face_flux(left, right, 2)

    def layer(z, state):
        after = face(z + 1, *state[:4])
        for f in range(FIELDS):
            total[f, z, blocks] = total[f, z, blocks] + (state[4][f] - after[4][f])
        return after

    lax.fori_loop(0, count, layer, face(0, here, half, ahead, ahead_step))


INNER = slice(0, 2)
EDGE = slice(2, 3)


def inner_kernel(first, own, second, w0, change):
    for z in range(QUARTER):
        index = (slice(None), slice(2 * z, 2 * z + 2))
        below, above = below_above(first, second, index)
        for base, piece in ((0, below), (QUARTER, own[index]), (2 * QUARTER, above)):
            values = [piece[f] for f in range(FIELDS)]
            for f, value in enumerate(primitives(values)):
                w0[f, base + z] = value
    rate_x(change, w0, QUARTER + HALO, INNER)
    rate_z(change, w0, QUARTER + HALO, INNER)


def first_step(layer, base, u1, w1, total):
    values = [base[f] + TIME_STEP * total[f, layer, INNER] for f in range(FIELDS)]
    for f, value in enumerate(values):
        u1[f, layer] = value
    for f, value in enumerate(primitives(values)):
        w1[f, layer, INNER] = value


def advance_kernel(
    held_counts, first, own, second, w0, inner, from_below, from_above, message,
    uh, wh, changeh, total, u1, w1, change, done,
):
    wide = QUARTER + HALO
    first_half = lax.broadcasted_iota(jnp.int32, (4, LANES), 1) < 64
    for field in range(FIELDS):
        for pair in range(4):
            rows = slice((pair % 2) * 4, (pair % 2) * 4 + 4)
            above = from_above[field, pair // 2, rows, :]
            below = from_below[field, pair // 2, rows, :]
            for z, halo in (
                (pair, jnp.where(first_half, above, pltpu.roll(below, 64, 1))),
                (pair + 4, jnp.where(first_half, pltpu.roll(above, 64, 1), below)),
            ):
                uh[field, z, 0, pl.ds(0, 4, stride=2), :] = halo
                uh[field, z, 0, pl.ds(1, 4, stride=2), :] = halo
    for f, value in enumerate(primitives([uh[f] for f in range(FIELDS)])):
        wh[f] = value

    rate_x(changeh, wh, QUARTER, slice(0, 1))
    rate_z(changeh, wh, QUARTER, slice(0, 1))

    def planes(step, carry):
        z = step * Y_LAYERS
        here, shifted = pl.ds(z, Y_LAYERS), pl.ds(z + 2, Y_LAYERS)
        prims = [[w0[f, shifted, 0], w0[f, shifted, 1], wh[f, here, 0]] for f in range(FIELDS)]
        changes = sweep_y(prims)
        for f in range(FIELDS):
            for i in range(2):
                total[f, here, i] = inner[f, here, i] + changes[f][i]
            total[f, here, 2] = changes[f][2]
        return carry

    lax.fori_loop(0, wide // Y_LAYERS, planes, 0)

    for z in range(QUARTER):
        index = (slice(None), slice(2 * z, 2 * z + 2))
        if z >= 2:
            layer, piece = z - 2, below_above(first, second, index)[0]
            first_step(layer, piece, u1, w1, total)
        else:
            layer, piece = z + 2 + QUARTER, below_above(first, second, index)[1]
            first_step(layer, piece, u1, w1, total)
        first_step(z + 2, own[index], u1, w1, total)
    for z in range(QUARTER):
        values = [
            uh[f, z + 2] + TIME_STEP * (total[f, z + 2, EDGE] + changeh[f, z])
            for f in range(FIELDS)
        ]
        for f, value in enumerate(primitives(values)):
            w1[f, z + 2, EDGE] = value

    rate_x(change, w1, QUARTER, INNER)
    rate_z(change, w1, QUARTER, INNER)

    def last_planes(step, carry):
        z = step * 4
        here, shifted = pl.ds(z, 4), pl.ds(z + 2, 4)
        changes = sweep_y([[w1[f, shifted, i] for i in range(3)] for f in range(FIELDS)])
        for f in range(FIELDS):
            for i in range(2):
                change[f, here, i] = change[f, here, i] + changes[f][i]
        return carry

    lax.fori_loop(0, 1, last_planes, 0)

    for z in range(QUARTER):
        for field in range(FIELDS):
            for block_y in range(2):
                value = 0.5 * own[field, 2 * z + block_y] + 0.5 * (
                    u1[field, z + 2, block_y] + TIME_STEP * change[field, z, block_y]
                )
                for xb in range(4):
                    done[block_y * 4 + xb, field, 2 * z : 2 * z + 2, :] = value[
                        2 * xb : 2 * xb + 2, :
                    ]

    row = held_counts[...]
    counts = [row[0, GROUP + device] for device in range(GROUP)]
    start = jnp.int32(0)
    for device in range(GROUP):
        for slot in range(SLOTS):
            key = jnp.minimum(start + slot, KEYS - 1)
            valid = slot < counts[device]
            for field in range(FIELDS):
                message[device, field, pl.ds(slot, ROWS, stride=SLOTS), :] = jnp.where(
                    valid, done[key, field], 0.0
                )
        start = start + counts[device]


def body(state_old, counts_old, counts_new):
    slabs = lax.axis_size("gz")
    places = lax.axis_size("blk")
    groups = places // GROUP
    slab = lax.axis_index("gz")
    group = lax.axis_index("blk") // GROUP

    def row_of(counts):
        return lax.dynamic_slice(counts, (slab, group, 0), (1, 1, GROUP)).reshape(GROUP)

    counts = jnp.concatenate([row_of(counts_old), row_of(counts_new)]).reshape(1, 2 * GROUP)
    members = [[g * GROUP + k for k in range(GROUP)] for g in range(groups)]

    def exchange(message):
        return lax.all_to_all(message, "blk", 0, 0, axis_index_groups=members)

    def along_y(value, by):
        route = [(i, (i + by * GROUP) % places) for i in range(places)]
        return lax.ppermute(value, "blk", route)

    def trade(value, offset):
        def device_of(quarter):
            g, k = divmod(quarter, GROUP)
            return g, k if g % 2 == 0 else GROUP - 1 - k

        route = []
        for quarter in range(slabs * GROUP):
            partner = (((quarter + offset) ^ 1) - offset) % (slabs * GROUP)
            (g, j), (to_g, to_j) = device_of(quarter), device_of(partner)
            for i in range(0, places, GROUP):
                route.append((g * places + i + j, to_g * places + i + to_j))
        return lax.ppermute(value, ("gz", "blk"), route)

    parts = f32(GROUP, FIELDS, LINES, LANES)
    slots = f32(FIELDS, GROUP * LINES, LANES)
    wide = QUARTER + HALO
    held = state_old.reshape(SLOTS, FIELDS, GROUP * ROWS, LANES).transpose(1, 2, 0, 3)
    held = held.reshape(slots.shape)
    arrivals = [pltpu.SemaphoreType.DMA((GROUP,))]
    received = exchange(call(split_kernel, parts, [VMEM])(held))

    own = call(gather_kernel, f32(FIELDS, 2 * QUARTER, ROWS, LANES), [VMEM, VMEM])(
        counts, received
    )
    first = trade(own, 0)
    second = trade(own, 1)

    edge = f32(FIELDS, 2, ROWS, LANES)
    lower, upper = call(edge_kernel, [edge, edge], [VMEM] * 3)(first, own, second)
    from_below = along_y(upper, 1)
    from_above = along_y(lower, -1)
    w0, inner = call(
        inner_kernel,
        [f32(FIELDS, wide + HALO, 2, ROWS, LANES), f32(FIELDS, wide, 2, ROWS, LANES)],
        [VMEM] * 3,
        flops=1 << 24,
    )(first, own, second)

    def work(*shape):
        return pltpu.VMEM((FIELDS,) + shape + (ROWS, LANES), jnp.float32)

    finished = call(
        advance_kernel,
        parts,
        [VMEM] * 8,
        [work(wide, 1), work(wide, 1), work(QUARTER, 1), work(wide, 3)]
        + [work(wide, 2), work(wide, 3), work(QUARTER, 2)]
        + [pltpu.VMEM((KEYS, FIELDS, ROWS, LANES), jnp.float32)],
        flops=1 << 24,
    )(counts, first, own, second, w0, inner, from_below, from_above)
    returned = exchange(finished)
    state = call(join_kernel, slots, [VMEM], arrivals, out=HBM)(returned)
    state = state.reshape(FIELDS, GROUP * ROWS, SLOTS, LANES).transpose(2, 0, 1, 3)
    return state.reshape(state_old.shape)


def solution(mesh):
    in_specs = (P("gz", "blk", None, None, None), P(), P())
    out_specs = P("gz", "blk", None, None, None)
    return jax.shard_map(body, mesh=mesh, in_specs=in_specs, out_specs=out_specs, check_vma=False)
```

```python
import jax
import jax.numpy as jnp
from jax import lax
from jax.experimental import pallas as pl
from jax.experimental.pallas import tpu as pltpu
from jax.sharding import PartitionSpec as P


FIELDS = 5
GROUP = 4
SLOTS = 4
KEYS = 8
ROWS = 8
LANES = 128
QUARTER = 4
HALO = 4
LINES = ROWS * SLOTS

TIME_STEP = 0.08
GAMMA = 1.4

VMEM = pl.BlockSpec(memory_space=pltpu.VMEM)
HBM = pl.BlockSpec(memory_space=pl.ANY)


def call(kernel, out_shapes, in_specs, scratch=(), flops=0, out=VMEM):
    return pl.pallas_call(
        kernel,
        out_shape=out_shapes,
        in_specs=in_specs,
        out_specs=jax.tree.map(lambda _: out, out_shapes),
        scratch_shapes=list(scratch),
        compiler_params=pltpu.CompilerParams(vmem_limit_bytes=24 << 20),
        cost_estimate=pl.CostEstimate(flops=flops, bytes_accessed=1 << 20, transcendentals=0),
    )


def f32(*shape):
    return jax.ShapeDtypeStruct(shape, jnp.float32)


def quarter_of(device):
    return jnp.where(lax.axis_index("gz") % 2 == 0, device, GROUP - 1 - device)


def even_quarter():
    return (lax.axis_index("blk") + lax.axis_index("gz")) % 2 == 0


def split_kernel(state, message):
    for device in range(GROUP):
        rows = pl.ds(pl.multiple_of(quarter_of(device) * LINES, LINES), LINES)
        message[device] = state[:, rows]


def join_kernel(received, state, arrived):
    copies = []
    for device in range(GROUP):
        rows = pl.ds(pl.multiple_of(quarter_of(device) * LINES, LINES), LINES)
        copies.append(
            pltpu.make_async_copy(received.at[device], state.at[:, rows], arrived.at[device])
        )
    for copy in copies:
        copy.start()
    for copy in copies:
        copy.wait()


def counts_here(held):
    row = held[lax.axis_index("gz")]
    device = lax.broadcasted_iota(jnp.int32, row.shape, 0)
    group = lax.broadcasted_iota(jnp.int32, row.shape, 1)
    here = jnp.where(group == lax.axis_index("blk") // GROUP, row, 0)
    return [jnp.sum(jnp.where(device == k, here, 0)) for k in range(GROUP)]


def place_of(counts, key):
    position = jnp.int32(0)
    first = jnp.int32(0)
    upto = jnp.int32(0)
    for device in range(GROUP - 1):
        upto = upto + counts[device]
        beyond = upto <= key
        position = position + beyond.astype(jnp.int32)
        first = jnp.where(beyond, upto, first)
    return position, jnp.clip(key - first, 0, SLOTS - 1)


def gather_kernel(held_counts, received, piece):
    counts = counts_here(held_counts)
    for block_y in range(2):
        for xb in range(4):
            device, slot = place_of(counts, block_y * 4 + xb)
            for field in range(FIELDS):
                block = received[device, field, pl.ds(slot, ROWS, stride=SLOTS), :]
                for z in range(QUARTER):
                    piece[field, z * 2 + block_y, 2 * xb : 2 * xb + 2, :] = block[
                        2 * z : 2 * z + 2
                    ]


def below_above(first, second, index):
    even = even_quarter()
    return (
        jnp.where(even, second[index], first[index]),
        jnp.where(even, first[index], second[index]),
    )


def edge_kernel(first, own, second, x_change, lower, upper):
    del x_change
    first_half = lax.broadcasted_iota(jnp.int32, (4, LANES), 1) < 64

    def rows(field, layer, block_y):
        rest = pl.ds(block_y, 4, stride=2)
        if layer < 0:
            return below_above(first, second, (field, 2 * (layer + HALO) + block_y, rest))[0]
        if layer >= QUARTER:
            return below_above(first, second, (field, 2 * (layer - QUARTER) + block_y, rest))[1]
        return own[field, 2 * layer + block_y, rest]

    for field in range(FIELDS):
        for pair in range(4):
            to = (pair % 2) * 4
            one, two = pair - 2, pair + 2
            lower[field, pair // 2, to : to + 4, :] = jnp.where(
                first_half, rows(field, one, 0), pltpu.roll(rows(field, two, 0), 64, 1)
            )
            upper[field, pair // 2, to : to + 4, :] = jnp.where(
                first_half, pltpu.roll(rows(field, one, 1), 64, 1), rows(field, two, 1)
            )


def minmod(left, right):
    return jnp.maximum(jnp.minimum(left, right), 0.0) + jnp.minimum(jnp.maximum(left, right), 0.0)


def primitives(conserved):
    density, mx, my, mz, energy = conserved
    inverse = 1.0 / density
    vx, vy, vz = mx * inverse, my * inverse, mz * inverse
    pressure = (GAMMA - 1.0) * (energy - 0.5 * (mx * vx + my * vy + mz * vz))
    return [density, vx, vy, vz, pressure]


def face_terms(primitive, normal):
    density, vx, vy, vz, pressure = primitive
    energy = pressure * (1.0 / (GAMMA - 1.0)) + (0.5 * density) * (vx * vx + vy * vy + vz * vz)
    conserved = [density, density * vx, density * vy, density * vz, energy]
    stiff = GAMMA * pressure
    sound = stiff * lax.rsqrt(stiff * density)
    return conserved, primitive[1 + normal], pressure, sound


def face_flux(left, right, normal):
    left_u, left_v, left_p, left_c = face_terms(left, normal)
    right_u, right_v, right_p, right_c = face_terms(right, normal)
    fastest = jnp.maximum(jnp.maximum(left_v + left_c, right_v + right_c), 0.0)
    slowest = jnp.minimum(jnp.minimum(left_v - left_c, right_v - right_c), 0.0)
    inverse = 1.0 / (fastest - slowest)
    plus = fastest * inverse
    minus = slowest * inverse
    left_weight = plus * (left_v - slowest)
    right_weight = minus * (right_v - fastest)
    left_push = plus * left_p
    right_push = minus * right_p
    fluxes = [left_weight * a - right_weight * b for a, b in zip(left_u, right_u)]
    fluxes[1 + normal] = fluxes[1 + normal] + (left_push - right_push)
    fluxes[4] = fluxes[4] + (left_push * left_v - right_push * right_v)
    return fluxes


def shift_x(value, amount):
    axis = value.ndim - 1
    x = lax.broadcasted_iota(jnp.int32, value.shape, axis) % 16
    if amount > 0:
        inner = pltpu.roll(value, 1, axis)
        outer = pltpu.roll(pltpu.roll(value, 2, axis - 1), LANES - 15, axis)
        return jnp.where(x == 0, outer, inner)
    inner = pltpu.roll(value, LANES - 1, axis)
    outer = pltpu.roll(pltpu.roll(value, ROWS - 2, axis - 1), 15, axis)
    return jnp.where(x == 15, outer, inner)


def shift_y(value, amount):
    shape = value[0].shape
    across, down = len(shape) - 1, len(shape) - 2
    lane = lax.broadcasted_iota(jnp.int32, shape, across)
    odd = lax.broadcasted_iota(jnp.int32, shape, down) % 2 == 1
    if amount > 0:
        moved = [pltpu.roll(v, 16, across) for v in value]
        upper = moved
        lower = [moved[i - 1] for i in range(3)]
        outer = lane < 16
    else:
        moved = [pltpu.roll(v, LANES - 16, across) for v in value]
        upper = [moved[(i + 1) % 3] for i in range(3)]
        lower = moved
        outer = lane >= LANES - 16
    edge = [
        jnp.where(odd, pltpu.roll(u, 1, down), pltpu.roll(l, ROWS - 1, down))
        for u, l in zip(upper, lower)
    ]
    return [jnp.where(outer, e, m) for e, m in zip(edge, moved)]


def sweep_x(primitive):
    ahead = [shift_x(q, -1) for q in primitive]
    steps = [b - q for q, b in zip(primitive, ahead)]
    half = [0.5 * minmod(shift_x(d, 1), d) for d in steps]
    left = [q + h for q, h in zip(primitive, half)]
    right = [shift_x(q - h, -1) for q, h in zip(primitive, half)]
    return [shift_x(f, 1) - f for f in face_flux(left, right, 0)]


def sweep_y(primitive):
    ahead = [shift_y(q, -1) for q in primitive]
    steps = [[b - a for a, b in zip(q, after)] for q, after in zip(primitive, ahead)]
    behind = [shift_y(d, 1) for d in steps]
    half = [[0.5 * minmod(a, b) for a, b in zip(p, d)] for p, d in zip(behind, steps)]
    beyond = [shift_y(h, -1) for h in half]
    fluxes = []
    for i in range(3):
        left = [q[i] + h[i] for q, h in zip(primitive, half)]
        right = [q[i] - h[i] for q, h in zip(ahead, beyond)]
        fluxes.append(face_flux(left, right, 1))
    out = []
    for flux in zip(*fluxes):
        out.append([b - f for b, f in zip(shift_y(list(flux), 1), flux)])
    return out


X_LAYERS = 4
Y_LAYERS = 4


def rate_x(total, prim, count, blocks, source=2, target=0, batch=X_LAYERS):
    def planes(step, carry):
        z = step * batch
        values = [prim[f, pl.ds(z + source, batch), blocks] for f in range(FIELDS)]
        for f, change in enumerate(sweep_x(values)):
            total[f, pl.ds(z + target, batch), blocks] = change
        return carry

    lax.fori_loop(0, count // batch, planes, 0)


def rate_z(total, prim, count, blocks):
    def load(z):
        return [prim[f, z, blocks] for f in range(FIELDS)]

    here, ahead = load(1), load(2)
    step = [h - b for h, b in zip(here, load(0))]
    ahead_step = [a - h for a, h in zip(ahead, here)]
    half = [0.5 * minmod(a, b) for a, b in zip(step, ahead_step)]

    def face(z, here, half, ahead, ahead_step):
        beyond = load(z + 3)
        beyond_step = [b - a for a, b in zip(ahead, beyond)]
        ahead_half = [0.5 * minmod(a, b) for a, b in zip(ahead_step, beyond_step)]
        left = [q + h for q, h in zip(here, half)]
        right = [q - h for q, h in zip(ahead, ahead_half)]
        return ahead, ahead_half, beyond, beyond_step, face_flux(left, right, 2)

    def layer(z, state):
        after = face(z + 1, *state[:4])
        for f in range(FIELDS):
            total[f, z, blocks] = total[f, z, blocks] + (state[4][f] - after[4][f])
        return after

    lax.fori_loop(0, count, layer, face(0, here, half, ahead, ahead_step))


INNER = slice(0, 2)
EDGE = slice(2, 3)


def own_kernel(own, prim, x_change):
    for z in range(QUARTER):
        values = [own[f, 2 * z : 2 * z + 2] for f in range(FIELDS)]
        for f, value in enumerate(primitives(values)):
            prim[f, z] = value
    rate_x(x_change, prim, QUARTER, INNER, 0, 0)


def inner_kernel(first, prim, x_change, second, w0, change):
    for z in range(HALO):
        index = (slice(None), slice(2 * z, 2 * z + 2))
        below, above = below_above(first, second, index)
        for base, piece in ((0, below), (HALO + QUARTER, above)):
            values = [piece[f] for f in range(FIELDS)]
            for f, value in enumerate(primitives(values)):
                w0[f, base + z] = value
    for f in range(FIELDS):
        w0[f, HALO : HALO + QUARTER] = prim[f]
        change[f, 2 : 2 + QUARTER] = x_change[f]
    rate_x(change, w0, 2, INNER, 2, 0, 2)
    rate_x(change, w0, 2, INNER, HALO + QUARTER, 2 + QUARTER, 2)
    rate_z(change, w0, QUARTER + HALO, INNER)


def first_step(layer, base, u1, w1, total):
    values = [base[f] + TIME_STEP * total[f, layer, INNER] for f in range(FIELDS)]
    for f, value in enumerate(values):
        u1[f, layer] = value
    for f, value in enumerate(primitives(values)):
        w1[f, layer, INNER] = value


def advance_kernel(
    held_counts, first, own, second, w0, inner, from_below, from_above, message,
    uh, wh, changeh, total, u1, w1, change, done,
):
    wide = QUARTER + HALO
    first_half = lax.broadcasted_iota(jnp.int32, (4, LANES), 1) < 64
    for field in range(FIELDS):
        for pair in range(4):
            rows = slice((pair % 2) * 4, (pair % 2) * 4 + 4)
            above = from_above[field, pair // 2, rows, :]
            below = from_below[field, pair // 2, rows, :]
            for z, halo in (
                (pair, jnp.where(first_half, above, pltpu.roll(below, 64, 1))),
                (pair + 4, jnp.where(first_half, pltpu.roll(above, 64, 1), below)),
            ):
                uh[field, z, 0, pl.ds(0, 4, stride=2), :] = halo
                uh[field, z, 0, pl.ds(1, 4, stride=2), :] = halo
    for f, value in enumerate(primitives([uh[f] for f in range(FIELDS)])):
        wh[f] = value

    rate_x(changeh, wh, QUARTER, slice(0, 1))
    rate_z(changeh, wh, QUARTER, slice(0, 1))

    def planes(step, carry):
        z = step * Y_LAYERS
        here, shifted = pl.ds(z, Y_LAYERS), pl.ds(z + 2, Y_LAYERS)
        prims = [[w0[f, shifted, 0], w0[f, shifted, 1], wh[f, here, 0]] for f in range(FIELDS)]
        changes = sweep_y(prims)
        for f in range(FIELDS):
            for i in range(2):
                total[f, here, i] = inner[f, here, i] + changes[f][i]
            total[f, here, 2] = changes[f][2]
        return carry

    lax.fori_loop(0, wide // Y_LAYERS, planes, 0)

    for z in range(QUARTER):
        index = (slice(None), slice(2 * z, 2 * z + 2))
        if z >= 2:
            layer, piece = z - 2, below_above(first, second, index)[0]
            first_step(layer, piece, u1, w1, total)
        else:
            layer, piece = z + 2 + QUARTER, below_above(first, second, index)[1]
            first_step(layer, piece, u1, w1, total)
        first_step(z + 2, own[index], u1, w1, total)
    for z in range(QUARTER):
        values = [
            uh[f, z + 2] + TIME_STEP * (total[f, z + 2, EDGE] + changeh[f, z])
            for f in range(FIELDS)
        ]
        for f, value in enumerate(primitives(values)):
            w1[f, z + 2, EDGE] = value

    rate_x(change, w1, QUARTER, INNER)
    rate_z(change, w1, QUARTER, INNER)

    def last_planes(step, carry):
        z = step * 4
        here, shifted = pl.ds(z, 4), pl.ds(z + 2, 4)
        changes = sweep_y([[w1[f, shifted, i] for i in range(3)] for f in range(FIELDS)])
        for f in range(FIELDS):
            for i in range(2):
                change[f, here, i] = change[f, here, i] + changes[f][i]
        return carry

    lax.fori_loop(0, 1, last_planes, 0)

    for z in range(QUARTER):
        for field in range(FIELDS):
            for block_y in range(2):
                value = 0.5 * own[field, 2 * z + block_y] + 0.5 * (
                    u1[field, z + 2, block_y] + TIME_STEP * change[field, z, block_y]
                )
                for xb in range(4):
                    done[block_y * 4 + xb, field, 2 * z : 2 * z + 2, :] = value[
                        2 * xb : 2 * xb + 2, :
                    ]

    counts = counts_here(held_counts)
    start = jnp.int32(0)
    for device in range(GROUP):
        for slot in range(SLOTS):
            key = jnp.minimum(start + slot, KEYS - 1)
            valid = slot < counts[device]
            for field in range(FIELDS):
                message[device, field, pl.ds(slot, ROWS, stride=SLOTS), :] = jnp.where(
                    valid, done[key, field], 0.0
                )
        start = start + counts[device]


def body(state_old, counts_old, counts_new):
    slabs = lax.axis_size("gz")
    places = lax.axis_size("blk")
    groups = places // GROUP
    members = [[g * GROUP + k for k in range(GROUP)] for g in range(groups)]

    def exchange(message):
        return lax.all_to_all(message, "blk", 0, 0, axis_index_groups=members)

    def along_y(value, by):
        route = [(i, (i + by * GROUP) % places) for i in range(places)]
        return lax.ppermute(value, "blk", route)

    def trade(value, offset):
        def device_of(quarter):
            g, k = divmod(quarter, GROUP)
            return g, k if g % 2 == 0 else GROUP - 1 - k

        route = []
        for quarter in range(slabs * GROUP):
            partner = (((quarter + offset) ^ 1) - offset) % (slabs * GROUP)
            (g, j), (to_g, to_j) = device_of(quarter), device_of(partner)
            for i in range(0, places, GROUP):
                route.append((g * places + i + j, to_g * places + i + to_j))
        return lax.ppermute(value, ("gz", "blk"), route)

    parts = f32(GROUP, FIELDS, LINES, LANES)
    slots = f32(FIELDS, GROUP * LINES, LANES)
    wide = QUARTER + HALO
    held = state_old.reshape(SLOTS, FIELDS, GROUP * ROWS, LANES).transpose(1, 2, 0, 3)
    held = held.reshape(slots.shape)
    arrivals = [pltpu.SemaphoreType.DMA((GROUP,))]
    received = exchange(call(split_kernel, parts, [VMEM])(held))

    own = call(gather_kernel, f32(FIELDS, 2 * QUARTER, ROWS, LANES), [VMEM, VMEM])(
        counts_old.transpose(0, 2, 1), received
    )
    first = trade(own, 0)
    second = trade(own, 1)
    block = f32(FIELDS, QUARTER, 2, ROWS, LANES)
    prim, x_change = call(own_kernel, [block, block], [VMEM], flops=1 << 24)(own)

    edge = f32(FIELDS, 2, ROWS, LANES)
    lower, upper = call(edge_kernel, [edge, edge], [VMEM] * 4)(
        first, own, second, x_change
    )
    from_below = along_y(upper, 1)
    from_above = along_y(lower, -1)
    w0, inner = call(
        inner_kernel,
        [f32(FIELDS, wide + HALO, 2, ROWS, LANES), f32(FIELDS, wide, 2, ROWS, LANES)],
        [VMEM] * 4,
        flops=1 << 24,
    )(first, prim, x_change, second)

    def work(*shape):
        return pltpu.VMEM((FIELDS,) + shape + (ROWS, LANES), jnp.float32)

    finished = call(
        advance_kernel,
        parts,
        [VMEM] * 8,
        [work(wide, 1), work(wide, 1), work(QUARTER, 1), work(wide, 3)]
        + [work(wide, 2), work(wide, 3), work(QUARTER, 2)]
        + [pltpu.VMEM((KEYS, FIELDS, ROWS, LANES), jnp.float32)],
        flops=1 << 24,
    )(counts_new.transpose(0, 2, 1), first, own, second, w0, inner, from_below, from_above)
    returned = exchange(finished)
    state = call(join_kernel, slots, [VMEM], arrivals, out=HBM)(returned)
    state = state.reshape(FIELDS, GROUP * ROWS, SLOTS, LANES).transpose(2, 0, 1, 3)
    return state.reshape(state_old.shape)


def solution(mesh):
    in_specs = (P("gz", "blk", None, None, None), P(), P())
    out_specs = P("gz", "blk", None, None, None)
    return jax.shard_map(body, mesh=mesh, in_specs=in_specs, out_specs=out_specs, check_vma=False)
```

```python
import jax
import jax.numpy as jnp
from jax import lax
from jax.experimental import pallas as pl
from jax.experimental.pallas import tpu as pltpu
from jax.sharding import PartitionSpec as P


FIELDS = 5
GROUP = 4
SLOTS = 4
KEYS = 8
ROWS = 8
LANES = 128
QUARTER = 4
HALO = 4
LINES = ROWS * SLOTS

TIME_STEP = 0.08
GAMMA = 1.4

VMEM = pl.BlockSpec(memory_space=pltpu.VMEM)
HBM = pl.BlockSpec(memory_space=pl.ANY)


def call(kernel, out_shapes, in_specs, scratch=(), flops=0, out=VMEM):
    return pl.pallas_call(
        kernel,
        out_shape=out_shapes,
        in_specs=in_specs,
        out_specs=jax.tree.map(lambda _: out, out_shapes),
        scratch_shapes=list(scratch),
        compiler_params=pltpu.CompilerParams(vmem_limit_bytes=24 << 20),
        cost_estimate=pl.CostEstimate(flops=flops, bytes_accessed=1 << 20, transcendentals=0),
    )


def f32(*shape):
    return jax.ShapeDtypeStruct(shape, jnp.float32)


def quarter_of(device):
    return jnp.where(lax.axis_index("gz") % 2 == 0, device, GROUP - 1 - device)


def even_quarter():
    return (lax.axis_index("blk") + lax.axis_index("gz")) % 2 == 0


def split_kernel(state, message):
    for device in range(GROUP):
        rows = pl.ds(pl.multiple_of(quarter_of(device) * LINES, LINES), LINES)
        message[device] = state[:, rows]


def join_kernel(received, state, arrived):
    copies = []
    for device in range(GROUP):
        rows = pl.ds(pl.multiple_of(quarter_of(device) * LINES, LINES), LINES)
        copies.append(
            pltpu.make_async_copy(received.at[device], state.at[:, rows], arrived.at[device])
        )
    for copy in copies:
        copy.start()
    for copy in copies:
        copy.wait()


def counts_here(held):
    row = held[lax.axis_index("gz")]
    device = lax.broadcasted_iota(jnp.int32, row.shape, 0)
    group = lax.broadcasted_iota(jnp.int32, row.shape, 1)
    here = jnp.where(group == lax.axis_index("blk") // GROUP, row, 0)
    return [jnp.sum(jnp.where(device == k, here, 0)) for k in range(GROUP)]


def place_of(counts, key):
    position = jnp.int32(0)
    first = jnp.int32(0)
    upto = jnp.int32(0)
    for device in range(GROUP - 1):
        upto = upto + counts[device]
        beyond = upto <= key
        position = position + beyond.astype(jnp.int32)
        first = jnp.where(beyond, upto, first)
    return position, jnp.clip(key - first, 0, SLOTS - 1)


def gather_kernel(held_counts, received, piece):
    counts = counts_here(held_counts)
    for block_y in range(2):
        for xb in range(4):
            device, slot = place_of(counts, block_y * 4 + xb)
            for field in range(FIELDS):
                block = received[device, field, pl.ds(slot, ROWS, stride=SLOTS), :]
                for z in range(QUARTER):
                    piece[field, z * 2 + block_y, 2 * xb : 2 * xb + 2, :] = block[
                        2 * z : 2 * z + 2
                    ]


def below_above(first, second, index):
    even = even_quarter()
    return (
        jnp.where(even, second[index], first[index]),
        jnp.where(even, first[index], second[index]),
    )


def edge_kernel(first, own, second, x_change, lower, upper):
    del x_change
    first_half = lax.broadcasted_iota(jnp.int32, (4, LANES), 1) < 64

    def rows(field, layer, block_y):
        rest = pl.ds(block_y, 4, stride=2)
        if layer < 0:
            return below_above(first, second, (field, 2 * (layer + HALO) + block_y, rest))[0]
        if layer >= QUARTER:
            return below_above(first, second, (field, 2 * (layer - QUARTER) + block_y, rest))[1]
        return own[field, 2 * layer + block_y, rest]

    for field in range(FIELDS):
        for pair in range(4):
            to = (pair % 2) * 4
            one, two = pair - 2, pair + 2
            lower[field, pair // 2, to : to + 4, :] = jnp.where(
                first_half, rows(field, one, 0), pltpu.roll(rows(field, two, 0), 64, 1)
            )
            upper[field, pair // 2, to : to + 4, :] = jnp.where(
                first_half, pltpu.roll(rows(field, one, 1), 64, 1), rows(field, two, 1)
            )


def minmod(left, right):
    return jnp.maximum(jnp.minimum(left, right), 0.0) + jnp.minimum(jnp.maximum(left, right), 0.0)


def primitives(conserved):
    density, mx, my, mz, energy = conserved
    inverse = 1.0 / density
    vx, vy, vz = mx * inverse, my * inverse, mz * inverse
    pressure = (GAMMA - 1.0) * (energy - 0.5 * (mx * vx + my * vy + mz * vz))
    return [density, vx, vy, vz, pressure]


def face_terms(primitive, normal):
    density, vx, vy, vz, pressure = primitive
    energy = pressure * (1.0 / (GAMMA - 1.0)) + (0.5 * density) * (vx * vx + vy * vy + vz * vz)
    conserved = [density, density * vx, density * vy, density * vz, energy]
    stiff = GAMMA * pressure
    sound = stiff * lax.rsqrt(stiff * density)
    return conserved, primitive[1 + normal], pressure, sound


def face_flux(left, right, normal):
    left_u, left_v, left_p, left_c = face_terms(left, normal)
    right_u, right_v, right_p, right_c = face_terms(right, normal)
    fastest = jnp.maximum(jnp.maximum(left_v + left_c, right_v + right_c), 0.0)
    slowest = jnp.minimum(jnp.minimum(left_v - left_c, right_v - right_c), 0.0)
    inverse = 1.0 / (fastest - slowest)
    plus = fastest * inverse
    minus = slowest * inverse
    left_weight = plus * (left_v - slowest)
    right_weight = minus * (right_v - fastest)
    left_push = plus * left_p
    right_push = minus * right_p
    fluxes = [left_weight * a - right_weight * b for a, b in zip(left_u, right_u)]
    fluxes[1 + normal] = fluxes[1 + normal] + (left_push - right_push)
    fluxes[4] = fluxes[4] + (left_push * left_v - right_push * right_v)
    return fluxes


def shift_x(value, amount):
    axis = value.ndim - 1
    x = lax.broadcasted_iota(jnp.int32, value.shape, axis) % 16
    if amount > 0:
        inner = pltpu.roll(value, 1, axis)
        outer = pltpu.roll(pltpu.roll(value, 2, axis - 1), LANES - 15, axis)
        return jnp.where(x == 0, outer, inner)
    inner = pltpu.roll(value, LANES - 1, axis)
    outer = pltpu.roll(pltpu.roll(value, ROWS - 2, axis - 1), 15, axis)
    return jnp.where(x == 15, outer, inner)


def shift_y(value, amount):
    shape = value[0].shape
    across, down = len(shape) - 1, len(shape) - 2
    lane = lax.broadcasted_iota(jnp.int32, shape, across)
    odd = lax.broadcasted_iota(jnp.int32, shape, down) % 2 == 1
    if amount > 0:
        moved = [pltpu.roll(v, 16, across) for v in value]
        upper = moved
        lower = moved[-1:] + moved[:-1]
        outer = lane < 16
    else:
        moved = [pltpu.roll(v, LANES - 16, across) for v in value]
        upper = moved[1:] + moved[:1]
        lower = moved
        outer = lane >= LANES - 16
    edge = [
        jnp.where(odd, pltpu.roll(u, 1, down), pltpu.roll(l, ROWS - 1, down))
        for u, l in zip(upper, lower)
    ]
    return [jnp.where(outer, e, m) for e, m in zip(edge, moved)]


def sweep_x(primitive):
    ahead = [shift_x(q, -1) for q in primitive]
    steps = [b - q for q, b in zip(primitive, ahead)]
    half = [0.5 * minmod(shift_x(d, 1), d) for d in steps]
    left = [q + h for q, h in zip(primitive, half)]
    right = [shift_x(q - h, -1) for q, h in zip(primitive, half)]
    return [shift_x(f, 1) - f for f in face_flux(left, right, 0)]


def sweep_y(primitive):
    ahead = [shift_y(q, -1) for q in primitive]
    steps = [[b - a for a, b in zip(q, after)] for q, after in zip(primitive, ahead)]
    behind = [shift_y(d, 1) for d in steps]
    half = [[0.5 * minmod(a, b) for a, b in zip(p, d)] for p, d in zip(behind, steps)]
    beyond = [shift_y(h, -1) for h in half]
    fluxes = []
    for i in range(len(primitive[0])):
        left = [q[i] + h[i] for q, h in zip(primitive, half)]
        right = [q[i] - h[i] for q, h in zip(ahead, beyond)]
        fluxes.append(face_flux(left, right, 1))
    out = []
    for flux in zip(*fluxes):
        out.append([b - f for b, f in zip(shift_y(list(flux), 1), flux)])
    return out


def sweep_strip(primitive):
    def shift(value, amount):
        return pltpu.roll(value, 16 if amount > 0 else LANES - 16, value.ndim - 1)

    ahead = [shift(q, -1) for q in primitive]
    steps = [b - q for q, b in zip(primitive, ahead)]
    half = [0.5 * minmod(shift(d, 1), d) for d in steps]
    left = [q + h for q, h in zip(primitive, half)]
    right = [shift(q - h, -1) for q, h in zip(primitive, half)]
    return [shift(f, 1) - f for f in face_flux(left, right, 1)]


def lane_and_odd():
    lane = lax.broadcasted_iota(jnp.int32, (ROWS, LANES), 1)
    return lane, lax.broadcasted_iota(jnp.int32, (ROWS, LANES), 0) % 2 == 1


def ends_of(low, high):
    _, odd = lane_and_odd()
    both = jnp.where(odd, high, low)
    return pltpu.roll(both, LANES // 2, both.ndim - 1)


def strip_halo():
    lane, odd = lane_and_odd()
    return odd == (lane >= LANES // 2)


def put_ends(low, high, strip):
    lane, odd = lane_and_odd()
    ends = pltpu.roll(strip, LANES // 2, strip.ndim - 1)
    low = jnp.where(jnp.logical_and(jnp.logical_not(odd), lane < 32), ends, low)
    return low, jnp.where(jnp.logical_and(odd, lane >= LANES - 32), ends, high)


def repeat(count, step):
    if count == 1:
        step(0, 0)
    else:
        lax.fori_loop(0, count, step, 0)


X_LAYERS = 4
Y_LAYERS = 4


def rate_x(total, prim, count, blocks, source=2, target=0, batch=X_LAYERS):
    def planes(step, carry):
        z = step * batch
        values = [prim[f, pl.ds(z + source, batch), blocks] for f in range(FIELDS)]
        for f, change in enumerate(sweep_x(values)):
            total[f, pl.ds(z + target, batch), blocks] = change
        return carry

    repeat(count // batch, planes)


def rate_z(total, prim, count, blocks):
    def load(z):
        return [prim[f, z, blocks] for f in range(FIELDS)]

    here, ahead = load(1), load(2)
    step = [h - b for h, b in zip(here, load(0))]
    ahead_step = [a - h for a, h in zip(ahead, here)]
    half = [0.5 * minmod(a, b) for a, b in zip(step, ahead_step)]

    def face(z, here, half, ahead, ahead_step):
        beyond = load(z + 3)
        beyond_step = [b - a for a, b in zip(ahead, beyond)]
        ahead_half = [0.5 * minmod(a, b) for a, b in zip(ahead_step, beyond_step)]
        left = [q + h for q, h in zip(here, half)]
        right = [q - h for q, h in zip(ahead, ahead_half)]
        return ahead, ahead_half, beyond, beyond_step, face_flux(left, right, 2)

    def layer(z, state):
        after = face(z + 1, *state[:4])
        for f in range(FIELDS):
            total[f, z, blocks] = total[f, z, blocks] + (state[4][f] - after[4][f])
        return after

    lax.fori_loop(0, count, layer, face(0, here, half, ahead, ahead_step), unroll=True)


INNER = slice(0, 2)
EDGE = slice(2, 3)


def rate_y(total, prim, count, source, target, batch):
    def planes(step, carry):
        here = pl.ds(step * batch + target, batch)
        shifted = pl.ds(step * batch + source, batch)
        changes = sweep_y([[prim[f, shifted, 0], prim[f, shifted, 1]] for f in range(FIELDS)])
        for f in range(FIELDS):
            for i in range(2):
                total[f, here, i] = changes[f][i]
        return carry

    repeat(count // batch, planes)


def own_kernel(own, prim, x_change, y_change):
    for z in range(QUARTER):
        values = [own[f, 2 * z : 2 * z + 2] for f in range(FIELDS)]
        for f, value in enumerate(primitives(values)):
            prim[f, z] = value
    rate_x(x_change, prim, QUARTER, INNER, 0, 0)
    rate_y(y_change, prim, QUARTER, 0, 0, QUARTER)


def inner_kernel(first, prim, x_change, y_change, second, change, along_y, w0):
    for z in range(HALO):
        index = (slice(None), slice(2 * z, 2 * z + 2))
        below, above = below_above(first, second, index)
        for base, piece in ((0, below), (HALO + QUARTER, above)):
            values = [piece[f] for f in range(FIELDS)]
            for f, value in enumerate(primitives(values)):
                w0[f, base + z] = value
    for f in range(FIELDS):
        w0[f, HALO : HALO + QUARTER] = prim[f]
        change[f, 2 : 2 + QUARTER] = x_change[f]
        along_y[f, 2 : 2 + QUARTER] = y_change[f]
    rate_x(change, w0, 2, INNER, 2, 0, 2)
    rate_x(change, w0, 2, INNER, HALO + QUARTER, 2 + QUARTER, 2)
    rate_y(along_y, w0, 2, 2, 0, 2)
    rate_y(along_y, w0, 2, HALO + QUARTER, 2 + QUARTER, 2)
    rate_z(change, w0, QUARTER + HALO, INNER)


def advance_kernel(
    held_counts, first, own, second, inner, along_y, from_below, from_above, message,
    us, ws, changes_h, u1s, u1, w1, w1s, change, done,
):
    wide = QUARTER + HALO
    first_half = lax.broadcasted_iota(jnp.int32, (4, LANES), 1) < 64
    for field in range(FIELDS):
        for pair in range(4):
            rows = slice((pair % 2) * 4, (pair % 2) * 4 + 4)
            above = from_above[field, pair // 2, rows, :]
            below = from_below[field, pair // 2, rows, :]
            for z, halo in (
                (pair, jnp.where(first_half, below, pltpu.roll(above, 64, 1))),
                (pair + 4, jnp.where(first_half, pltpu.roll(below, 64, 1), above)),
            ):
                us[field, z, 0, pl.ds(0, 4, stride=2), :] = halo
                us[field, z, 0, pl.ds(1, 4, stride=2), :] = halo

    def u0_of(layer):
        if 2 <= layer < 2 + QUARTER:
            return own[:, 2 * (layer - 2) : 2 * (layer - 2) + 2]
        if layer < 2:
            return below_above(first, second, (slice(None), slice(2 * layer + 4, 2 * layer + 6)))[0]
        at = 2 * (layer - 2 - QUARTER)
        return below_above(first, second, (slice(None), slice(at, at + 2)))[1]

    halo = strip_halo()
    for layer in range(wide):
        base = u0_of(layer)
        values = [
            jnp.where(halo, us[f, layer, 0], ends_of(base[f, 0], base[f, 1]))
            for f in range(FIELDS)
        ]
        for f, value in enumerate(values):
            us[f, layer, 0] = value
        for f, value in enumerate(primitives(values)):
            ws[f, layer, 0] = value

    rate_x(changes_h, ws, QUARTER, slice(0, 1))
    rate_z(changes_h, ws, QUARTER, slice(0, 1))

    sweeps = sweep_strip([ws[f, :, 0] for f in range(FIELDS)])
    for f in range(FIELDS):
        u1s[f, :, 0] = sweeps[f]

    for layer in range(wide):
        base = u0_of(layer)
        low, high, strip = [], [], []
        for f in range(FIELDS):
            rest = ends_of(inner[f, layer, 0], inner[f, layer, 1])
            if 2 <= layer < 2 + QUARTER:
                rest = jnp.where(halo, changes_h[f, layer - 2, 0], rest)
            strip.append(us[f, layer, 0] + TIME_STEP * (rest + u1s[f, layer, 0]))
            ends = [
                base[f, i] + TIME_STEP * (inner[f, layer, i] + along_y[f, layer, i])
                for i in range(2)
            ]
            ends = put_ends(ends[0], ends[1], strip[f])
            low.append(ends[0])
            high.append(ends[1])
            u1[f, layer, 0], u1[f, layer, 1] = ends
        for f, value in enumerate(primitives(low)):
            w1[f, layer, 0] = value
        for f, value in enumerate(primitives(high)):
            w1[f, layer, 1] = value
        if 2 <= layer < 2 + QUARTER:
            strip = [jnp.where(halo, s, ends_of(l, h)) for s, l, h in zip(strip, low, high)]
            for f, value in enumerate(primitives(strip)):
                w1s[f, layer - 2] = value

    rate_x(change, w1, QUARTER, INNER)
    rate_z(change, w1, QUARTER, INNER)
    shifted = slice(2, 2 + QUARTER)
    sweeps = sweep_y([[w1[f, shifted, 0], w1[f, shifted, 1]] for f in range(FIELDS)])
    strips_y = sweep_strip([w1s[f] for f in range(FIELDS)])
    for field in range(FIELDS):
        sweeps_y = put_ends(sweeps[field][0], sweeps[field][1], strips_y[field])
        for block_y in range(2):
            for z in range(QUARTER):
                rate = change[field, z, block_y] + sweeps_y[block_y][z]
                value = 0.5 * own[field, 2 * z + block_y] + 0.5 * (
                    u1[field, z + 2, block_y] + TIME_STEP * rate
                )
                for xb in range(4):
                    done[block_y * 4 + xb, field, 2 * z : 2 * z + 2, :] = value[
                        2 * xb : 2 * xb + 2, :
                    ]

    counts = counts_here(held_counts)
    start = jnp.int32(0)
    for device in range(GROUP):
        for slot in range(SLOTS):
            key = jnp.minimum(start + slot, KEYS - 1)
            valid = slot < counts[device]
            for field in range(FIELDS):
                message[device, field, pl.ds(slot, ROWS, stride=SLOTS), :] = jnp.where(
                    valid, done[key, field], 0.0
                )
        start = start + counts[device]


def body(state_old, counts_old, counts_new):
    slabs = lax.axis_size("gz")
    places = lax.axis_size("blk")
    groups = places // GROUP
    members = [[g * GROUP + k for k in range(GROUP)] for g in range(groups)]

    def exchange(message):
        return lax.all_to_all(message, "blk", 0, 0, axis_index_groups=members)

    def along_y(value, by):
        route = [(i, (i + by * GROUP) % places) for i in range(places)]
        return lax.ppermute(value, "blk", route)

    def trade(value, offset):
        def device_of(quarter):
            g, k = divmod(quarter, GROUP)
            return g, k if g % 2 == 0 else GROUP - 1 - k

        route = []
        for quarter in range(slabs * GROUP):
            partner = (((quarter + offset) ^ 1) - offset) % (slabs * GROUP)
            (g, j), (to_g, to_j) = device_of(quarter), device_of(partner)
            for i in range(0, places, GROUP):
                route.append((g * places + i + j, to_g * places + i + to_j))
        return lax.ppermute(value, ("gz", "blk"), route)

    parts = f32(GROUP, FIELDS, LINES, LANES)
    slots = f32(FIELDS, GROUP * LINES, LANES)
    wide = QUARTER + HALO
    held = state_old.reshape(SLOTS, FIELDS, GROUP * ROWS, LANES).transpose(1, 2, 0, 3)
    held = held.reshape(slots.shape)
    arrivals = [pltpu.SemaphoreType.DMA((GROUP,))]
    received = exchange(call(split_kernel, parts, [VMEM])(held))

    own = call(gather_kernel, f32(FIELDS, 2 * QUARTER, ROWS, LANES), [VMEM, VMEM])(
        counts_old.transpose(0, 2, 1), received
    )
    first = trade(own, 0)
    second = trade(own, 1)
    block = f32(FIELDS, QUARTER, 2, ROWS, LANES)
    prim, x_change, y_change = call(own_kernel, [block] * 3, [VMEM], flops=1 << 24)(own)

    edge = f32(FIELDS, 2, ROWS, LANES)
    lower, upper = call(edge_kernel, [edge, edge], [VMEM] * 4)(
        first, own, second, x_change
    )
    from_below = along_y(upper, 1)
    from_above = along_y(lower, -1)

    def work(*shape):
        return pltpu.VMEM((FIELDS,) + shape + (ROWS, LANES), jnp.float32)

    change = f32(FIELDS, wide, 2, ROWS, LANES)
    inner, inner_y = call(
        inner_kernel, [change, change], [VMEM] * 5, [work(wide + HALO, 2)], flops=1 << 24
    )(first, prim, x_change, y_change, second)
    finished = call(
        advance_kernel,
        parts,
        [VMEM] * 8,
        [work(wide, 1), work(wide, 1), work(QUARTER, 1), work(wide, 1)]
        + [work(wide, 2), work(wide, 2), work(QUARTER), work(QUARTER, 2)]
        + [pltpu.VMEM((KEYS, FIELDS, ROWS, LANES), jnp.float32)],
        flops=1 << 24,
    )(counts_new.transpose(0, 2, 1), first, own, second, inner, inner_y, from_below, from_above)
    returned = exchange(finished)
    state = call(join_kernel, slots, [VMEM], arrivals, out=HBM)(returned)
    state = state.reshape(FIELDS, GROUP * ROWS, SLOTS, LANES).transpose(2, 0, 1, 3)
    return state.reshape(state_old.shape)


def solution(mesh):
    in_specs = (P("gz", "blk", None, None, None), P(), P())
    out_specs = P("gz", "blk", None, None, None)
    return jax.shard_map(body, mesh=mesh, in_specs=in_specs, out_specs=out_specs, check_vma=False)
```

```python
import jax
import jax.numpy as jnp
from jax import lax
from jax.experimental import pallas as pl
from jax.experimental.pallas import tpu as pltpu
from jax.sharding import PartitionSpec as P


FIELDS = 5
GROUP = 4
SLOTS = 4
KEYS = 8
ROWS = 8
LANES = 128
QUARTER = 4
HALO = 4
LINES = ROWS * SLOTS

TIME_STEP = 0.08
GAMMA = 1.4

VMEM = pl.BlockSpec(memory_space=pltpu.VMEM)
HBM = pl.BlockSpec(memory_space=pl.ANY)


def call(kernel, out_shapes, in_specs, scratch=(), flops=0, out=VMEM):
    return pl.pallas_call(
        kernel,
        out_shape=out_shapes,
        in_specs=in_specs,
        out_specs=jax.tree.map(lambda _: out, out_shapes),
        scratch_shapes=list(scratch),
        compiler_params=pltpu.CompilerParams(vmem_limit_bytes=24 << 20),
        cost_estimate=pl.CostEstimate(flops=flops, bytes_accessed=1 << 20, transcendentals=0),
    )


def f32(*shape):
    return jax.ShapeDtypeStruct(shape, jnp.float32)


def quarter_of(device):
    return jnp.where(lax.axis_index("gz") % 2 == 0, device, GROUP - 1 - device)


def even_quarter():
    return (lax.axis_index("blk") + lax.axis_index("gz")) % 2 == 0


def split_kernel(state, message):
    for device in range(GROUP):
        rows = pl.ds(pl.multiple_of(quarter_of(device) * LINES, LINES), LINES)
        message[device] = state[:, rows]


def join_kernel(received, state, arrived):
    copies = []
    for device in range(GROUP):
        rows = pl.ds(pl.multiple_of(quarter_of(device) * LINES, LINES), LINES)
        copies.append(
            pltpu.make_async_copy(received.at[device], state.at[:, rows], arrived.at[device])
        )
    for copy in copies:
        copy.start()
    for copy in copies:
        copy.wait()


def counts_here(held):
    row = held[lax.axis_index("gz")]
    device = lax.broadcasted_iota(jnp.int32, row.shape, 0)
    group = lax.broadcasted_iota(jnp.int32, row.shape, 1)
    here = jnp.where(group == lax.axis_index("blk") // GROUP, row, 0)
    return [jnp.sum(jnp.where(device == k, here, 0)) for k in range(GROUP)]


def place_of(counts, key):
    position = jnp.int32(0)
    first = jnp.int32(0)
    upto = jnp.int32(0)
    for device in range(GROUP - 1):
        upto = upto + counts[device]
        beyond = upto <= key
        position = position + beyond.astype(jnp.int32)
        first = jnp.where(beyond, upto, first)
    return position, jnp.clip(key - first, 0, SLOTS - 1)


def gather_kernel(held_counts, received, piece):
    counts = counts_here(held_counts)
    for block_y in range(2):
        for xb in range(4):
            device, slot = place_of(counts, block_y * 4 + xb)
            for field in range(FIELDS):
                block = received[device, field, pl.ds(slot, ROWS, stride=SLOTS), :]
                for z in range(QUARTER):
                    piece[field, z * 2 + block_y, 2 * xb : 2 * xb + 2, :] = block[
                        2 * z : 2 * z + 2
                    ]


def below_above(first, second, index):
    even = even_quarter()
    return (
        jnp.where(even, second[index], first[index]),
        jnp.where(even, first[index], second[index]),
    )


def edge_kernel(first, own, second, x_change, lower, upper):
    del x_change
    first_half = lax.broadcasted_iota(jnp.int32, (4, LANES), 1) < 64

    def rows(field, layer, block_y):
        rest = pl.ds(block_y, 4, stride=2)
        if layer < 0:
            return below_above(first, second, (field, 2 * (layer + HALO) + block_y, rest))[0]
        if layer >= QUARTER:
            return below_above(first, second, (field, 2 * (layer - QUARTER) + block_y, rest))[1]
        return own[field, 2 * layer + block_y, rest]

    for field in range(FIELDS):
        for pair in range(4):
            to = (pair % 2) * 4
            one, two = pair - 2, pair + 2
            lower[field, pair // 2, to : to + 4, :] = jnp.where(
                first_half, rows(field, one, 0), pltpu.roll(rows(field, two, 0), 64, 1)
            )
            upper[field, pair // 2, to : to + 4, :] = jnp.where(
                first_half, pltpu.roll(rows(field, one, 1), 64, 1), rows(field, two, 1)
            )


def minmod(left, right):
    return jnp.maximum(jnp.minimum(left, right), 0.0) + jnp.minimum(jnp.maximum(left, right), 0.0)


def primitives(conserved):
    density, mx, my, mz, energy = conserved
    inverse = 1.0 / density
    vx, vy, vz = mx * inverse, my * inverse, mz * inverse
    pressure = (GAMMA - 1.0) * (energy - 0.5 * (mx * vx + my * vy + mz * vz))
    return [density, vx, vy, vz, pressure]


def face_terms(primitive, normal):
    density, vx, vy, vz, pressure = primitive
    energy = pressure * (1.0 / (GAMMA - 1.0)) + (0.5 * density) * (vx * vx + vy * vy + vz * vz)
    conserved = [density, density * vx, density * vy, density * vz, energy]
    stiff = GAMMA * pressure
    sound = stiff * lax.rsqrt(stiff * density)
    return conserved, primitive[1 + normal], pressure, sound


def face_flux(left, right, normal):
    left_u, left_v, left_p, left_c = face_terms(left, normal)
    right_u, right_v, right_p, right_c = face_terms(right, normal)
    fastest = jnp.maximum(jnp.maximum(left_v + left_c, right_v + right_c), 0.0)
    slowest = jnp.minimum(jnp.minimum(left_v - left_c, right_v - right_c), 0.0)
    inverse = 1.0 / (fastest - slowest)
    plus = fastest * inverse
    minus = slowest * inverse
    left_weight = plus * (left_v - slowest)
    right_weight = minus * (right_v - fastest)
    left_push = plus * left_p
    right_push = minus * right_p
    fluxes = [left_weight * a - right_weight * b for a, b in zip(left_u, right_u)]
    fluxes[1 + normal] = fluxes[1 + normal] + (left_push - right_push)
    fluxes[4] = fluxes[4] + (left_push * left_v - right_push * right_v)
    return fluxes


def shift_x(value, amount):
    axis = value.ndim - 1
    x = lax.broadcasted_iota(jnp.int32, value.shape, axis) % 16
    if amount > 0:
        inner = pltpu.roll(value, 1, axis)
        outer = pltpu.roll(pltpu.roll(value, 2, axis - 1), LANES - 15, axis)
        return jnp.where(x == 0, outer, inner)
    inner = pltpu.roll(value, LANES - 1, axis)
    outer = pltpu.roll(pltpu.roll(value, ROWS - 2, axis - 1), 15, axis)
    return jnp.where(x == 15, outer, inner)


def shift_y(value, amount):
    shape = value[0].shape
    across, down = len(shape) - 1, len(shape) - 2
    lane = lax.broadcasted_iota(jnp.int32, shape, across)
    odd = lax.broadcasted_iota(jnp.int32, shape, down) % 2 == 1
    if amount > 0:
        moved = [pltpu.roll(v, 16, across) for v in value]
        upper = moved
        lower = moved[-1:] + moved[:-1]
        outer = lane < 16
    else:
        moved = [pltpu.roll(v, LANES - 16, across) for v in value]
        upper = moved[1:] + moved[:1]
        lower = moved
        outer = lane >= LANES - 16
    edge = [
        jnp.where(odd, pltpu.roll(u, 1, down), pltpu.roll(l, ROWS - 1, down))
        for u, l in zip(upper, lower)
    ]
    return [jnp.where(outer, e, m) for e, m in zip(edge, moved)]


def sweep_x(primitive):
    ahead = [shift_x(q, -1) for q in primitive]
    steps = [b - q for q, b in zip(primitive, ahead)]
    half = [0.5 * minmod(shift_x(d, 1), d) for d in steps]
    left = [q + h for q, h in zip(primitive, half)]
    right = [shift_x(q - h, -1) for q, h in zip(primitive, half)]
    return [shift_x(f, 1) - f for f in face_flux(left, right, 0)]


def sweep_y(primitive):
    ahead = [shift_y(q, -1) for q in primitive]
    steps = [[b - a for a, b in zip(q, after)] for q, after in zip(primitive, ahead)]
    behind = [shift_y(d, 1) for d in steps]
    half = [[0.5 * minmod(a, b) for a, b in zip(p, d)] for p, d in zip(behind, steps)]
    beyond = [shift_y(h, -1) for h in half]
    fluxes = []
    for i in range(len(primitive[0])):
        left = [q[i] + h[i] for q, h in zip(primitive, half)]
        right = [q[i] - h[i] for q, h in zip(ahead, beyond)]
        fluxes.append(face_flux(left, right, 1))
    out = []
    for flux in zip(*fluxes):
        out.append([b - f for b, f in zip(shift_y(list(flux), 1), flux)])
    return out


def sweep_strip(primitive):
    def shift(value, amount):
        return pltpu.roll(value, 16 if amount > 0 else LANES - 16, value.ndim - 1)

    ahead = [shift(q, -1) for q in primitive]
    steps = [b - q for q, b in zip(primitive, ahead)]
    half = [0.5 * minmod(shift(d, 1), d) for d in steps]
    left = [q + h for q, h in zip(primitive, half)]
    right = [shift(q - h, -1) for q, h in zip(primitive, half)]
    return [shift(f, 1) - f for f in face_flux(left, right, 1)]


def lane_and_odd():
    lane = lax.broadcasted_iota(jnp.int32, (ROWS, LANES), 1)
    return lane, lax.broadcasted_iota(jnp.int32, (ROWS, LANES), 0) % 2 == 1


def ends_of(low, high):
    _, odd = lane_and_odd()
    both = jnp.where(odd, high, low)
    return pltpu.roll(both, LANES // 2, both.ndim - 1)


def strip_halo():
    lane, odd = lane_and_odd()
    return odd == (lane >= LANES // 2)


def put_ends(low, high, strip):
    lane, odd = lane_and_odd()
    ends = pltpu.roll(strip, LANES // 2, strip.ndim - 1)
    low = jnp.where(jnp.logical_and(jnp.logical_not(odd), lane < 32), ends, low)
    return low, jnp.where(jnp.logical_and(odd, lane >= LANES - 32), ends, high)


def repeat(count, step):
    if count == 1:
        step(0, 0)
    else:
        lax.fori_loop(0, count, step, 0)


X_LAYERS = 4
Y_LAYERS = 4


def rate_x(total, prim, count, blocks, source=2, target=0, batch=X_LAYERS):
    def planes(step, carry):
        z = step * batch
        values = [prim[f, pl.ds(z + source, batch), blocks] for f in range(FIELDS)]
        for f, change in enumerate(sweep_x(values)):
            total[f, pl.ds(z + target, batch), blocks] = change
        return carry

    repeat(count // batch, planes)


def rate_z(total, prim, count, blocks):
    def load(z):
        return [prim[f, z, blocks] for f in range(FIELDS)]

    here, ahead = load(1), load(2)
    step = [h - b for h, b in zip(here, load(0))]
    ahead_step = [a - h for a, h in zip(ahead, here)]
    half = [0.5 * minmod(a, b) for a, b in zip(step, ahead_step)]

    def face(z, here, half, ahead, ahead_step):
        beyond = load(z + 3)
        beyond_step = [b - a for a, b in zip(ahead, beyond)]
        ahead_half = [0.5 * minmod(a, b) for a, b in zip(ahead_step, beyond_step)]
        left = [q + h for q, h in zip(here, half)]
        right = [q - h for q, h in zip(ahead, ahead_half)]
        return ahead, ahead_half, beyond, beyond_step, face_flux(left, right, 2)

    def layer(z, state):
        after = face(z + 1, *state[:4])
        for f in range(FIELDS):
            total[f, z, blocks] = total[f, z, blocks] + (state[4][f] - after[4][f])
        return after

    lax.fori_loop(0, count, layer, face(0, here, half, ahead, ahead_step), unroll=True)


INNER = slice(0, 2)
EDGE = slice(2, 3)


def rate_y(total, prim, count, source, target, batch):
    def planes(step, carry):
        here = pl.ds(step * batch + target, batch)
        shifted = pl.ds(step * batch + source, batch)
        changes = sweep_y([[prim[f, shifted, 0], prim[f, shifted, 1]] for f in range(FIELDS)])
        for f in range(FIELDS):
            for i in range(2):
                total[f, here, i] = changes[f][i]
        return carry

    repeat(count // batch, planes)


def own_kernel(own, prim, x_change, y_change):
    for z in range(QUARTER):
        values = [own[f, 2 * z : 2 * z + 2] for f in range(FIELDS)]
        for f, value in enumerate(primitives(values)):
            prim[f, z] = value
    rate_x(x_change, prim, QUARTER, INNER, 0, 0)
    rate_y(y_change, prim, QUARTER, 0, 0, QUARTER)


def inner_kernel(
    first, own, prim, x_change, y_change, second, middle, strips, rests, change, along_y, w0
):
    def u0_of(layer):
        if 2 <= layer < 2 + QUARTER:
            return own[:, 2 * (layer - 2) : 2 * (layer - 2) + 2]
        if layer < 2:
            return below_above(first, second, (slice(None), slice(2 * layer + 4, 2 * layer + 6)))[0]
        at = 2 * (layer - 2 - QUARTER)
        return below_above(first, second, (slice(None), slice(at, at + 2)))[1]

    for z in range(HALO):
        index = (slice(None), slice(2 * z, 2 * z + 2))
        below, above = below_above(first, second, index)
        for base, piece in ((0, below), (HALO + QUARTER, above)):
            values = [piece[f] for f in range(FIELDS)]
            for f, value in enumerate(primitives(values)):
                w0[f, base + z] = value
    for f in range(FIELDS):
        w0[f, HALO : HALO + QUARTER] = prim[f]
        change[f, 2 : 2 + QUARTER] = x_change[f]
        along_y[f, 2 : 2 + QUARTER] = y_change[f]
    rate_x(change, w0, 2, INNER, 2, 0, 2)
    rate_x(change, w0, 2, INNER, HALO + QUARTER, 2 + QUARTER, 2)
    rate_y(along_y, w0, 2, 2, 0, 2)
    rate_y(along_y, w0, 2, HALO + QUARTER, 2 + QUARTER, 2)
    rate_z(change, w0, QUARTER + HALO, INNER)

    for layer in range(QUARTER + HALO):
        base = u0_of(layer)
        for f in range(FIELDS):
            middle[f, layer] = base[f] + TIME_STEP * (change[f, layer] + along_y[f, layer])
            strips[f, layer] = ends_of(base[f, 0], base[f, 1])
            rests[f, layer] = ends_of(change[f, layer, 0], change[f, layer, 1])


def advance_kernel(
    held_counts, own, middle, strips, rests, from_below, from_above, message,
    us, ws, changes_h, u1s, u1, w1, w1s, change, done,
):
    wide = QUARTER + HALO
    first_half = lax.broadcasted_iota(jnp.int32, (4, LANES), 1) < 64
    for field in range(FIELDS):
        for pair in range(4):
            rows = slice((pair % 2) * 4, (pair % 2) * 4 + 4)
            above = from_above[field, pair // 2, rows, :]
            below = from_below[field, pair // 2, rows, :]
            for z, halo in (
                (pair, jnp.where(first_half, below, pltpu.roll(above, 64, 1))),
                (pair + 4, jnp.where(first_half, pltpu.roll(below, 64, 1), above)),
            ):
                us[field, z, 0, pl.ds(0, 4, stride=2), :] = halo
                us[field, z, 0, pl.ds(1, 4, stride=2), :] = halo

    halo = strip_halo()
    for layer in range(wide):
        values = [jnp.where(halo, us[f, layer, 0], strips[f, layer]) for f in range(FIELDS)]
        for f, value in enumerate(values):
            us[f, layer, 0] = value
        for f, value in enumerate(primitives(values)):
            ws[f, layer, 0] = value

    rate_x(changes_h, ws, QUARTER, slice(0, 1))
    rate_z(changes_h, ws, QUARTER, slice(0, 1))

    sweeps = sweep_strip([ws[f, :, 0] for f in range(FIELDS)])
    for f in range(FIELDS):
        u1s[f, :, 0] = sweeps[f]

    for layer in range(wide):
        low, high, strip = [], [], []
        for f in range(FIELDS):
            rest = rests[f, layer]
            if 2 <= layer < 2 + QUARTER:
                rest = jnp.where(halo, changes_h[f, layer - 2, 0], rest)
            strip.append(us[f, layer, 0] + TIME_STEP * (rest + u1s[f, layer, 0]))
            ends = put_ends(middle[f, layer, 0], middle[f, layer, 1], strip[f])
            low.append(ends[0])
            high.append(ends[1])
            u1[f, layer, 0], u1[f, layer, 1] = ends
        for f, value in enumerate(primitives(low)):
            w1[f, layer, 0] = value
        for f, value in enumerate(primitives(high)):
            w1[f, layer, 1] = value
        if 2 <= layer < 2 + QUARTER:
            strip = [jnp.where(halo, s, ends_of(l, h)) for s, l, h in zip(strip, low, high)]
            for f, value in enumerate(primitives(strip)):
                w1s[f, layer - 2] = value

    rate_x(change, w1, QUARTER, INNER)
    rate_z(change, w1, QUARTER, INNER)
    shifted = slice(2, 2 + QUARTER)
    sweeps = sweep_y([[w1[f, shifted, 0], w1[f, shifted, 1]] for f in range(FIELDS)])
    strips_y = sweep_strip([w1s[f] for f in range(FIELDS)])
    for field in range(FIELDS):
        sweeps_y = put_ends(sweeps[field][0], sweeps[field][1], strips_y[field])
        for block_y in range(2):
            for z in range(QUARTER):
                rate = change[field, z, block_y] + sweeps_y[block_y][z]
                value = 0.5 * own[field, 2 * z + block_y] + 0.5 * (
                    u1[field, z + 2, block_y] + TIME_STEP * rate
                )
                for xb in range(4):
                    done[block_y * 4 + xb, field, 2 * z : 2 * z + 2, :] = value[
                        2 * xb : 2 * xb + 2, :
                    ]

    counts = counts_here(held_counts)
    start = jnp.int32(0)
    for device in range(GROUP):
        for slot in range(SLOTS):
            key = jnp.minimum(start + slot, KEYS - 1)
            valid = slot < counts[device]
            for field in range(FIELDS):
                message[device, field, pl.ds(slot, ROWS, stride=SLOTS), :] = jnp.where(
                    valid, done[key, field], 0.0
                )
        start = start + counts[device]


def body(state_old, counts_old, counts_new):
    slabs = lax.axis_size("gz")
    places = lax.axis_size("blk")
    groups = places // GROUP
    members = [[g * GROUP + k for k in range(GROUP)] for g in range(groups)]

    def exchange(message):
        return lax.all_to_all(message, "blk", 0, 0, axis_index_groups=members)

    def along_y(value, by):
        route = [(i, (i + by * GROUP) % places) for i in range(places)]
        return lax.ppermute(value, "blk", route)

    def trade(value, offset):
        def device_of(quarter):
            g, k = divmod(quarter, GROUP)
            return g, k if g % 2 == 0 else GROUP - 1 - k

        route = []
        for quarter in range(slabs * GROUP):
            partner = (((quarter + offset) ^ 1) - offset) % (slabs * GROUP)
            (g, j), (to_g, to_j) = device_of(quarter), device_of(partner)
            for i in range(0, places, GROUP):
                route.append((g * places + i + j, to_g * places + i + to_j))
        return lax.ppermute(value, ("gz", "blk"), route)

    parts = f32(GROUP, FIELDS, LINES, LANES)
    slots = f32(FIELDS, GROUP * LINES, LANES)
    wide = QUARTER + HALO
    held = state_old.reshape(SLOTS, FIELDS, GROUP * ROWS, LANES).transpose(1, 2, 0, 3)
    held = held.reshape(slots.shape)
    arrivals = [pltpu.SemaphoreType.DMA((GROUP,))]
    received = exchange(call(split_kernel, parts, [VMEM])(held))

    own = call(gather_kernel, f32(FIELDS, 2 * QUARTER, ROWS, LANES), [VMEM, VMEM])(
        counts_old.transpose(0, 2, 1), received
    )
    first = trade(own, 0)
    second = trade(own, 1)
    block = f32(FIELDS, QUARTER, 2, ROWS, LANES)
    prim, x_change, y_change = call(own_kernel, [block] * 3, [VMEM], flops=1 << 24)(own)

    edge = f32(FIELDS, 2, ROWS, LANES)
    lower, upper = call(edge_kernel, [edge, edge], [VMEM] * 4)(
        first, own, second, x_change
    )
    from_below = along_y(upper, 1)
    from_above = along_y(lower, -1)

    def work(*shape):
        return pltpu.VMEM((FIELDS,) + shape + (ROWS, LANES), jnp.float32)

    change = f32(FIELDS, wide, 2, ROWS, LANES)
    strip = f32(FIELDS, wide, ROWS, LANES)
    middle, strips, rests = call(
        inner_kernel,
        [change, strip, strip],
        [VMEM] * 6,
        [work(wide, 2), work(wide, 2), work(wide + HALO, 2)],
        flops=1 << 24,
    )(first, own, prim, x_change, y_change, second)
    finished = call(
        advance_kernel,
        parts,
        [VMEM] * 7,
        [work(wide, 1), work(wide, 1), work(QUARTER, 1), work(wide, 1)]
        + [work(wide, 2), work(wide, 2), work(QUARTER), work(QUARTER, 2)]
        + [pltpu.VMEM((KEYS, FIELDS, ROWS, LANES), jnp.float32)],
        flops=1 << 24,
    )(counts_new.transpose(0, 2, 1), own, middle, strips, rests, from_below, from_above)
    returned = exchange(finished)
    state = call(join_kernel, slots, [VMEM], arrivals, out=HBM)(returned)
    state = state.reshape(FIELDS, GROUP * ROWS, SLOTS, LANES).transpose(2, 0, 1, 3)
    return state.reshape(state_old.shape)


def solution(mesh):
    in_specs = (P("gz", "blk", None, None, None), P(), P())
    out_specs = P("gz", "blk", None, None, None)
    return jax.shard_map(body, mesh=mesh, in_specs=in_specs, out_specs=out_specs, check_vma=False)
```
